256 devices in a mesh: blk: 64 (over z, x, core), reg: 4 (over y).
Axes of the slice: x: 4, y: 4, z: 8, core: 2. Of those that a mesh axis runs over, the one named last changes fastest.
Arguments:
- coefficients: bfloat16 [256, 2048, 256], P('blk'), may hold values from -0.1875 to 0.1875
- legendre: bfloat16 [256, 64, 4, 2, 2048], P('blk', None, 'reg'), may hold values from -0.125 to 0.125
- harmonic_orders: int32 [256], replicated, may hold values from 0 to 2047, as said below
- observed: float32 [512, 4096], P(('blk', 'reg')), may hold values from -6 to 6
- hole_rows: int32 [512, 4096], P(('blk', 'reg')), may hold values from -1 to 511, as said below
- boundary: int32 [64, 4, 256], P('blk'), may hold values from 0 to 32767, as said below
- tile_owner: int32 [64, 4], P('blk'), may hold values from 0 to 3, each once within a row
- kriging: bfloat16 [64, 4, 512, 256], P('blk', 'reg'), may hold values from -0.375 to 0.375
Outputs:
- filled: bfloat16 [128, 512, 4096], P(None, ('blk', 'reg'))
The draws below stay inside these ranges and needn't reach their ends.
Inputs may be any that keep to these rules, and one draw needn't show every extreme that they name: `harmonic_orders`: distinct orders; both 0 and 2047 occur. `hole_rows`: the holes of region k of group b lie in cycles (b * 4 + k) * 2 to (b * 4 + k + 1) * 2 - 1; a region with n hole pixels numbers them 0 to n - 1, once each; in every group one region has exactly 512 hole pixels. `boundary`: the 256 pixels of a region are distinct, lie in its group's cycles, and none is a hole pixel; entries i with i // 64 = d lie in cycles (b * 4 + d) * 2 to (b * 4 + d + 1) * 2 - 1. `tile_owner`: each row is a permutation of 0 to 3.
All inputs are finite; a program needn't handle non-finite values.
Results may differ from the reference program's by a relative error of at most 0.0032.
Values may be sent and summed in bfloat16 or wider, within the bound.
No kernel may reach another device: no remote copies, remote signals or barrier semaphores. Data moves between devices by JAX's collectives and lax.ppermute only.
A program may use at most 64 MiB of HBM per device.

```python
import math
import jax
import jax.numpy as jnp
from jax import lax

L = 2048
NPHI = 4096
NB = 256
HMAX = 512
NSIM = 128
R_DEV = 2
MTOT = 256
CYCLES = 512
N_BLK = 64
N_REG = 4


def permuted_pixels(key):
    device_pixels = R_DEV * NPHI
    keys_all = jax.random.split(key, N_BLK * N_REG)
    place = HMAX + (N_REG - 1) * (NB // N_REG)

    def one_shuffle(one_key):
        rest = jax.random.permutation(one_key, device_pixels - 1).astype(jnp.int32)
        last = jnp.array([device_pixels - 1], dtype=jnp.int32)
        return jnp.concatenate([rest[:place], last, rest[place:]])
    shuffles = jax.vmap(one_shuffle)(keys_all)
    return shuffles.reshape(N_BLK, N_REG, device_pixels).astype(jnp.int32)


def draw_hole_rows(key, part):
    shuffled = permuted_pixels(key)
    key = jax.random.fold_in(key, 11)
    count_key, full_key = jax.random.split(key)
    counts = jax.random.randint(count_key, (N_BLK, N_REG), HMAX // 8, HMAX // 2 + 1)
    full_region = jax.random.randint(full_key, (N_BLK, 1), 0, N_REG)
    counts = jnp.where(jnp.arange(N_REG, dtype=jnp.int32)[None, :] == full_region, HMAX, counts)
    ranks = jnp.argsort(shuffled, axis=-1, stable=True).astype(jnp.int32)
    values = jnp.where(ranks < counts[:, :, None], ranks, -1)
    return values.reshape(N_BLK * N_REG * R_DEV, NPHI).astype(jnp.int32)


def draw_boundary(key, part):
    shuffled = permuted_pixels(key)
    device_pixels = R_DEV * NPHI
    positions = jnp.arange(NB, dtype=jnp.int32)
    sources = jnp.broadcast_to((positions // (NB // N_REG))[None, None, :], (N_BLK, N_REG, NB)).astype(jnp.int32)
    offsets = HMAX + jnp.arange(N_REG, dtype=jnp.int32)[:, None] * NB + positions[None, :]
    offsets = jnp.broadcast_to(offsets[None], (N_BLK, N_REG, NB))
    groups = jnp.broadcast_to(jnp.arange(N_BLK, dtype=jnp.int32)[:, None, None], (N_BLK, N_REG, NB))
    chosen = shuffled[groups, sources, offsets]
    return (sources * device_pixels + chosen).astype(jnp.int32)


def draw_harmonic_orders(key, part):
    key = jax.random.fold_in(key, 37)
    pick_key, order_key = jax.random.split(key)
    highest = NPHI // 2 - 1
    middle = 1 + jax.random.permutation(pick_key, highest - 1)[:MTOT - 2]
    values = jnp.concatenate([jnp.array([0, highest], dtype=jnp.int32), middle.astype(jnp.int32)])
    return jax.random.permutation(order_key, values).astype(jnp.int32)


def steps_of(key, shape, pieces, least, top_value):
    gain, own = 1.0, jax.random.fold_in(key, 6)
    for axis_at, shards_of in pieces:
        draws = jnp.exp(jax.random.uniform(jax.random.fold_in(own, axis_at), (shards_of,), jnp.float32, least / len(pieces), top_value / len(pieces)))
        gain = gain * jnp.repeat(draws, shape[axis_at] // shards_of).reshape([-1 if axis == axis_at else 1 for axis in range(len(shape))])
    return gain


def centred(own_key, extent, spread, limit, cuts=(), kind=jnp.bfloat16):
    entries = jax.random.normal(own_key, extent, jnp.float32) * spread
    if len(cuts) > 0:
        entries = steps_of(own_key, extent, cuts, -0.22, 0.18) * entries
    return jnp.clip(entries, min=-limit, max=limit).astype(kind)


def setup_inputs(seed: int = 0) -> dict:
    splits = jax.random.split(jax.random.key(seed), 9)
    return {
        "coefficients": centred(splits[0], (MTOT, L, 2 * NSIM), (0.5 / MTOT ** 0.5), 0.1875, ((0, 64),)),
        "legendre": centred(splits[1], (MTOT, N_BLK, N_REG, R_DEV, L), L ** -0.5, 0.125, ((0, 64), (2, 4))),
        "harmonic_orders": draw_harmonic_orders(jax.random.fold_in(splits[8], 71), 0),
        "observed": centred(splits[3], (CYCLES, NPHI), 1.0, 6.0, ((0, 256),), jnp.float32),
        "hole_rows": draw_hole_rows(jax.random.fold_in(splits[8], 71), 0),
        "boundary": draw_boundary(jax.random.fold_in(splits[8], 71), 0),
        "tile_owner": jax.vmap(lambda own: jax.random.permutation(own, N_REG))(jax.random.split(splits[6], N_BLK)).reshape((N_BLK, N_REG)).astype(jnp.int32),
        "kriging": centred(splits[7], (N_BLK, N_REG, HMAX, NB), NB ** -0.5, 0.375, ((0, 64), (1, 4))),
    }


def phase_table(harmonic_orders, cycle_pixels):
    columns = jnp.arange(cycle_pixels, dtype=jnp.int32)
    phase_steps = (harmonic_orders[:, None] * columns[None, :]) % cycle_pixels
    angles = phase_steps.astype(jnp.float32) * (2.0 * math.pi / cycle_pixels)
    weights = jnp.where(harmonic_orders == 0, 1.0, 2.0).astype(jnp.float32)[:, None]
    return jnp.stack([weights * jnp.cos(angles), -weights * jnp.sin(angles)]).astype(jnp.bfloat16)


def reference(coefficients, legendre, harmonic_orders, observed, hole_rows, boundary, tile_owner, kriging):
    phases = phase_table(harmonic_orders, NPHI).astype(jnp.float32)
    stacked = legendre.reshape(MTOT, CYCLES, L)

    def legendre_sum(operands):
        return jnp.dot(operands[0], operands[1], preferred_element_type=jnp.float32).astype(jnp.bfloat16)

    spectra = lax.map(legendre_sum, (stacked, coefficients))
    group_cycles = N_REG * R_DEV
    grouped = spectra.reshape(MTOT, N_BLK, group_cycles, 2, NSIM).transpose(1, 0, 2, 3, 4)
    sky_obs = observed.reshape(N_BLK, group_cycles, NPHI)
    group_holes = hole_rows.reshape(N_BLK, group_cycles, NPHI)
    region_of = (jnp.arange(group_cycles, dtype=jnp.int32) // R_DEV)[:, None]

    def one_group(group_items):
        spectra_block, observed_part, hole_part, edge_list, owners, tile_part = group_items
        sky_map = jnp.einsum("mrcs,cmp->srp", spectra_block.astype(jnp.float32), phases).astype(jnp.bfloat16)
        pixels_flat = sky_map.reshape(NSIM, group_cycles * NPHI)
        observed_flat = observed_part.reshape(group_cycles * NPHI)
        edge_index = edge_list.reshape(N_REG * NB)
        residual = observed_flat[edge_index][None, :] - pixels_flat[:, edge_index].astype(jnp.float32)
        residual = residual.astype(jnp.bfloat16).reshape(NSIM, N_REG, NB).transpose(1, 0, 2)
        chosen = tile_part[owners]
        correction = jnp.einsum("khi,ksi->ksh", chosen.astype(jnp.float32), residual.astype(jnp.float32)).astype(jnp.bfloat16)
        table_rows = correction.transpose(1, 0, 2).reshape(NSIM, N_REG * HMAX)
        hole_index = jnp.where(hole_part >= 0, region_of * HMAX + hole_part, 0).reshape(group_cycles * NPHI)
        picked = jnp.take(table_rows, hole_index, axis=1).reshape(NSIM, group_cycles, NPHI)
        filled = jnp.where((hole_part >= 0)[None], sky_map.astype(jnp.float32) + picked.astype(jnp.float32), observed_part[None].astype(jnp.float32))
        return filled.astype(jnp.bfloat16)

    result = lax.map(one_group, (grouped, sky_obs, group_holes, boundary, tile_owner, kriging))
    return result.transpose(1, 0, 2, 3).reshape(NSIM, CYCLES, NPHI)
```

```python
import functools

import jax
import jax.numpy as jnp
from jax import lax
from jax.experimental import pallas as pl
from jax.experimental.pallas import tpu as pltpu
from jax.sharding import PartitionSpec as P

BF = jnp.bfloat16
F32 = jnp.float32
I32 = jnp.int32
NBLK = 64
NREG = 4
NM = 4
L = 2048
KT = L // 128
NPHI = 4096
NG = 2 * NPHI // 128
NB = 256
SLOTS = NB // NREG
HMAX = 512
NS = 128
NK = NBLK * 16
MB = 1024 * 1024
ROUND = 12582912.0
COS = (
    0.9999999890590234,
    -19.739204499453898,
    64.93911745989367,
    -85.45013953084099,
    60.16763095056212,
    -25.967599246900118,
    6.528658158989,
)


def vmem():
    return pl.BlockSpec(memory_space=pltpu.VMEM)


def smem():
    return pl.BlockSpec(memory_space=pltpu.SMEM)


def anywhere():
    return pl.BlockSpec(memory_space=pl.ANY)


def params(mib):
    return pltpu.CompilerParams(vmem_limit_bytes=mib * MB)


def iota(shape, axis):
    return lax.broadcasted_iota(I32, shape, axis)


def dot(a, b):
    return jnp.dot(a, b, preferred_element_type=F32)


def dot_nt(a, b):
    return lax.dot_general(a, b, (((1,), (1,)), ((), ())), preferred_element_type=F32)


def legendre_kernel(leg, coef, out, legv, coefv, resv, lsem, csem, osem):
    def coef_copy(m):
        return pltpu.make_async_copy(coef.at[m], coefv.at[m], csem.at[m])

    for m in range(NM):
        for k in range(KT):
            pltpu.make_async_copy(leg.at[m, :, k], legv.at[m, k], lsem.at[m]).start()
        coef_copy(m).start()
    for m in range(NM):
        pltpu.make_async_copy(legv.at[m], legv.at[m], lsem.at[m]).wait()
        coef_copy(m).wait()
        total = jnp.zeros((2 * NBLK, 2 * NS), F32)
        for k in range(KT // 2):
            pair = [legv.at[m, 2 * k + i].reshape(2 * NBLK, 128)[...] for i in range(2)]
            total += dot(jnp.concatenate(pair, axis=1), coefv[m, k * 256 : (k + 1) * 256, :])
        rounded = total.astype(BF)
        for c in range(2):
            resv.at[m, c].reshape(2 * NBLK, 128)[...] = rounded[:, c * 128 : (c + 1) * 128]
            pltpu.make_async_copy(resv.at[m, c], out.at[:, c, m], osem).start()
    pltpu.make_async_copy(resv, resv, osem).wait()


def legendre_sums(legendre, coefficients):
    view = legendre.reshape(NM, NBLK, 2, KT, 128).transpose(0, 1, 3, 2, 4)
    return pl.pallas_call(
        legendre_kernel,
        out_shape=jax.ShapeDtypeStruct((NBLK, 2, NM, 2, 128), BF),
        in_specs=[anywhere(), anywhere()],
        out_specs=anywhere(),
        scratch_shapes=[
            pltpu.VMEM((NM, KT, NBLK, 2, 128), BF),
            pltpu.VMEM((NM, L, 2 * NS), BF),
            pltpu.VMEM((NM, 2, NBLK, 2, 128), BF),
            pltpu.SemaphoreType.DMA((NM,)),
            pltpu.SemaphoreType.DMA((NM,)),
            pltpu.SemaphoreType.DMA,
        ],
        compiler_params=params(60),
        cost_estimate=pl.CostEstimate(flops=2 * NM * 128 * L * 256, bytes_accessed=6 * MB, transcendentals=0),
        name="legendre_sums",
    )(view, coefficients)


def prepare_kernel(reg, holes, observed, boundary, orders, pb, ph, obsb, grp, lan, obsm, amat, bmat, pcol, rcol, rows):
    me = reg[0]
    h = holes[...].reshape(NG, 128)
    obs = observed[...].reshape(NG, 128)
    obsm[...] = jnp.where(h >= 0, 0.0, obs).astype(BF)

    hi, lo = h >> 4, h & 15
    a_iota, b_iota, lane = iota((32, 128), 0), iota((16, 128), 0), iota((32, 128), 1).astype(F32)
    for g in range(NG):
        hit = a_iota == hi[g : g + 1, :]
        at = pl.ds(g * 128, 128)
        amat[0:32, at] = jnp.where(hit, float(g + 1), 0.0).astype(BF)
        amat[32:64, at] = jnp.where(hit, lane, 0.0).astype(BF)
        bmat[:, at] = jnp.where(b_iota == lo[g : g + 1, :], 1.0, 0.0).astype(BF)
    tall = dot_nt(amat[...], bmat[...]).astype(BF)
    wide = dot_nt(bmat[...], amat[...]).astype(BF)
    pick = (iota((HMAX, 32), 0) // 16 == iota((HMAX, 32), 1)).astype(F32).astype(BF)
    low = iota((HMAX, 16), 0) % 16 == iota((HMAX, 16), 1)
    g1 = jnp.sum(jnp.where(low, dot(pick, tall[0:32]), 0.0), axis=1, keepdims=True)
    lh = jnp.sum(jnp.where(low, dot(pick, tall[32:64]), 0.0), axis=1, keepdims=True)
    pick_t = (iota((32, HMAX), 1) // 16 == iota((32, HMAX), 0)).astype(F32).astype(BF)
    low_t = iota((16, HMAX), 1) % 16 == iota((16, HMAX), 0)
    g1_row = jnp.sum(jnp.where(low_t, dot(wide[:, 0:32], pick_t), 0.0), axis=0, keepdims=True)
    grp[...] = jnp.where((iota((NG, HMAX), 0) + 1).astype(F32) == g1_row, 1.0, 0.0).astype(BF)
    lan[...] = jnp.where(iota((HMAX, 128), 1).astype(F32) == lh, 1.0, 0.0).astype(BF)
    gh = g1 - 1.0
    tile_h = jnp.floor(gh * 0.5)
    pcol[NB:, :] = jnp.broadcast_to(tile_h * 128.0 + lh, (HMAX, 128))
    rcol[NB:, :] = jnp.broadcast_to(gh - 2.0 * tile_h, (HMAX, 128))

    mine = iota((SLOTS, NB), 1) == iota((SLOTS, NB), 0) + me * SLOTS
    cols = []
    for d in range(NREG):
        line = boundary[pl.ds(lax.rem(me + d, NREG), 1), :].astype(F32)
        cols.append(jnp.sum(jnp.where(mine, line, 0.0), axis=1, keepdims=True))
    u = jnp.concatenate(cols, axis=0) - (me * (2 * NPHI)).astype(F32)
    rb = jnp.where(u >= float(NPHI), 1.0, 0.0)
    p = u - rb * float(NPHI)
    tile_b = jnp.floor(p * (1.0 / 128.0))
    lane_b = p - tile_b * 128.0
    pcol[0:NB, :] = jnp.broadcast_to(p, (NB, 128))
    rcol[0:NB, :] = jnp.broadcast_to(rb, (NB, 128))
    one = jnp.where(iota((NB, NG), 1).astype(F32) == 2.0 * tile_b + rb, 1.0, 0.0).astype(BF)
    first = obs.astype(BF)
    rest = obs - first.astype(F32)
    second = rest.astype(BF)
    third = (rest - second.astype(F32)).astype(BF)
    value = dot(one, first) + dot(one, second) + dot(one, third)
    value = jnp.where(iota((NB, 128), 1).astype(F32) == lane_b, value, 0.0)
    obsb[...] = jnp.broadcast_to(jnp.sum(value, axis=1, keepdims=True), (NB, 128))

    line = jnp.broadcast_to(orders[...], (8, 256))
    split = jnp.concatenate([(line >> 3).astype(F32), (line & 7).astype(F32)], axis=0).astype(BF)
    at = iota((256, NK), 1)
    spread = (iota((256, NK), 0) == (at >> 4) * 4 + ((at & 7) >> 1)).astype(F32).astype(BF)
    both = dot(split, spread)
    order = both[0:8] * 8.0 + both[8:16]
    at = iota((8, NK), 1)
    rows[0] = order * (1.0 / NPHI)
    rows[1] = ((at >> 3) & 1).astype(F32) * 0.25
    rows[2] = (at & 1).astype(F32)
    rows[3] = jnp.where(order == 0.0, 1.0, 2.0)

    def phases(out, base):
        def step(i, _):
            at = pl.multiple_of(i * 16, 16)
            pc = pcol[pl.ds(base + at, 16), :]
            rc = rcol[pl.ds(base + at, 16), :]
            for t in range(NK // 128):
                ls = slice(t * 128, (t + 1) * 128)
                turn = pc * rows[0, 0:1, ls] + rows[1, 0:1, ls]
                turn = turn - ((turn + ROUND) - ROUND)
                z = turn * turn
                value = jnp.full((16, 128), COS[-1], F32)
                for c in COS[-2::-1]:
                    value = value * z + c
                weight = jnp.where(rc == rows[2, 0:1, ls], rows[3, 0:1, ls], 0.0)
                out[pl.ds(at, 16), ls] = (value * weight).astype(BF)
            return 0

        lax.fori_loop(0, out.shape[0] // 16, step, 0)

    phases(pb, 0)
    phases(ph, NB)


def prepare(reg, holes, observed, boundary, orders):
    shapes = [
        ((NB, NK), BF),
        ((HMAX, NK), BF),
        ((NB, 128), F32),
        ((NG, HMAX), BF),
        ((HMAX, 128), BF),
        ((NG, 128), BF),
    ]
    return pl.pallas_call(
        prepare_kernel,
        out_shape=[jax.ShapeDtypeStruct(s, t) for s, t in shapes],
        in_specs=[smem()] + [vmem()] * 4,
        out_specs=[vmem()] * 6,
        scratch_shapes=[
            pltpu.VMEM((64, 2 * NPHI), BF),
            pltpu.VMEM((16, 2 * NPHI), BF),
            pltpu.VMEM((NB + HMAX, 128), F32),
            pltpu.VMEM((NB + HMAX, 128), F32),
            pltpu.VMEM((4, 8, NK), F32),
        ],
        compiler_params=params(30),
        cost_estimate=pl.CostEstimate(flops=20_000_000, bytes_accessed=8 * MB, transcendentals=0),
        name="prepare",
    )(reg, holes, observed, boundary, orders)


def residual_kernel(spectra, pb, obsb, own, to1, to2, to3):
    sky = dot(pb[...], spectra[...]).astype(BF).astype(F32)
    residual = (obsb[...] - sky).astype(BF)
    for d, ref in enumerate((own, to1, to2, to3)):
        ref[...] = residual[d * SLOTS : (d + 1) * SLOTS, :]


def residuals(spectra, pb, obsb):
    return pl.pallas_call(
        residual_kernel,
        out_shape=[jax.ShapeDtypeStruct((SLOTS, NS), BF)] * NREG,
        in_specs=[vmem()] * 3,
        out_specs=[vmem()] * NREG,
        compiler_params=params(30),
        cost_estimate=pl.CostEstimate(flops=2 * NB * NK * NS, bytes_accessed=MB, transcendentals=0),
        name="residuals",
    )(spectra, pb, obsb)


def hole_kernel(reg, owners, spectra, ph, tile0, tile1, tile2, tile3, after, sky, tile):
    del after
    sky[...] = dot(ph[...], spectra[...]).astype(BF)
    me = reg[0]
    away = lax.rem(me - owners[0, me] + NREG, NREG)
    for d, ref in enumerate((tile0, tile1, tile2, tile3)):

        @pl.when(away == d)
        def _(ref=ref):
            tile[...] = ref[...]


def hole_sky(reg, owners, spectra, ph, tiles, after):
    return pl.pallas_call(
        hole_kernel,
        out_shape=[jax.ShapeDtypeStruct((HMAX, NS), BF), jax.ShapeDtypeStruct((HMAX, NB), BF)],
        in_specs=[smem(), smem()] + [vmem()] * 6 + [anywhere()],
        out_specs=[vmem()] * 2,
        compiler_params=params(30),
        cost_estimate=pl.CostEstimate(flops=2 * HMAX * NK * NS, bytes_accessed=2 * MB, transcendentals=0),
        name="hole_sky",
    )(reg, owners, spectra, ph, *tiles, after)


CHUNK = 8


def fill_kernel(reg, own, from1, from2, from3, tile, sky, grp, lan, obsm, out, edge, xt, outv, sem):
    me = reg[0]
    for d, ref in enumerate((own, from1, from2, from3)):
        source = lax.rem(me - d + NREG, NREG)
        edge[pl.ds(pl.multiple_of(source * SLOTS, SLOTS), SLOTS), :] = ref[...]
    correction = dot(tile[...], edge[...]).astype(BF)
    holes = (sky[...].astype(F32) + correction.astype(F32)).astype(BF).astype(F32)
    xt[...] = holes.T
    groups = grp[...]
    lanes = lan[...]
    base = obsm[...]

    def copy(i):
        at = pl.ds(pl.multiple_of(i * (CHUNK * NG), CHUNK * NG), CHUNK * NG)
        return pltpu.make_async_copy(outv.at[at], out.at[at], sem)

    def step(i, _):
        parts = []
        for j in range(CHUNK):
            line = xt[pl.ds(i * CHUNK + j, 1), :].astype(BF)
            parts.append(groups * line)
        got = dot(jnp.concatenate(parts, axis=0), lanes).astype(BF)
        for j in range(CHUNK):
            at = pl.multiple_of(i * (CHUNK * NG) + j * NG, NG)
            outv[pl.ds(at, NG), :] = got[j * NG : (j + 1) * NG] + base
        copy(i).start()
        return 0

    lax.fori_loop(0, NS // CHUNK, step, 0)
    pltpu.make_async_copy(outv, outv, sem).wait()


def fill(reg, edges, tile, sky, grp, lan, obsm):
    return pl.pallas_call(
        fill_kernel,
        out_shape=jax.ShapeDtypeStruct((NS * NG, 128), BF),
        in_specs=[smem()] + [vmem()] * 9,
        out_specs=anywhere(),
        scratch_shapes=[
            pltpu.VMEM((NB, NS), BF),
            pltpu.VMEM((NS, HMAX), F32),
            pltpu.VMEM((NS * NG, 128), BF),
            pltpu.SemaphoreType.DMA,
        ],
        compiler_params=params(60),
        cost_estimate=pl.CostEstimate(flops=2 * NS * NG * HMAX * 128, bytes_accessed=3 * MB, transcendentals=0),
        name="fill",
    )(reg, *edges, tile, sky, grp, lan, obsm)


def by_lane_tile(x):
    return x.reshape(2, NPHI // 128, 128).transpose(1, 0, 2)


def shifted(x, d):
    return lax.ppermute(x, "reg", [(i, (i + d) % NREG) for i in range(NREG)])


def body(coefficients, legendre, harmonic_orders, observed, hole_rows, boundary, tile_owner, kriging):
    reg = lax.axis_index("reg").astype(I32).reshape(1)
    sums = legendre_sums(legendre, coefficients)
    spectra = lax.all_to_all(sums, "blk", split_axis=0, concat_axis=0, tiled=True).reshape(NK, 128)
    pb, ph, obsb, grp, lan, obsm = prepare(
        reg, by_lane_tile(hole_rows), by_lane_tile(observed), boundary.reshape(NREG, NB), harmonic_orders.reshape(1, -1)
    )
    tile = kriging.reshape(HMAX, NB)
    tiles = [tile] + [shifted(tile, d) for d in (1, 2, 3)]
    own, *away = residuals(spectra, pb, obsb)
    edges = [own] + [shifted(x, d + 1) for d, x in enumerate(away)]
    sky, my_tile = hole_sky(reg, tile_owner, spectra, ph, tiles, own)
    out = fill(reg, edges, my_tile, sky, grp, lan, obsm)
    return out.reshape(NS, NPHI // 128, 2, 128).transpose(0, 2, 1, 3).reshape(NS, 2, NPHI)


def solution(mesh):
    return jax.shard_map(
        body,
        mesh=mesh,
        in_specs=(
            P("blk", None, None),
            P("blk", None, "reg", None, None),
            P(),
            P(("blk", "reg"), None),
            P(("blk", "reg"), None),
            P("blk", None, None),
            P("blk", None),
            P("blk", "reg", None, None),
        ),
        out_specs=P(None, ("blk", "reg"), None),
        check_vma=False,
    )
```

```python
import functools

import jax
import jax.numpy as jnp
from jax import lax
from jax.experimental import pallas as pl
from jax.experimental.pallas import tpu as pltpu
from jax.sharding import PartitionSpec as P

BF = jnp.bfloat16
F32 = jnp.float32
I32 = jnp.int32
NBLK = 64
NREG = 4
NM = 4
L = 2048
KT = L // 128
NPHI = 4096
NT = NPHI // 128
NG = 2 * NT
NB = 256
SLOTS = NB // NREG
HMAX = 512
NS = 128
NK = NBLK * 16
MB = 1024 * 1024
ROUND = 12582912.0
COS = (
    0.9999999890590234,
    -19.739204499453898,
    64.93911745989367,
    -85.45013953084099,
    60.16763095056212,
    -25.967599246900118,
    6.528658158989,
)


def vmem():
    return pl.BlockSpec(memory_space=pltpu.VMEM)


def smem():
    return pl.BlockSpec(memory_space=pltpu.SMEM)


def anywhere():
    return pl.BlockSpec(memory_space=pl.ANY)


def params(mib):
    return pltpu.CompilerParams(vmem_limit_bytes=mib * MB)


def iota(shape, axis):
    return lax.broadcasted_iota(I32, shape, axis)


def dot(a, b):
    return jnp.dot(a, b, preferred_element_type=F32)


def dot_nt(a, b):
    return lax.dot_general(a, b, (((1,), (1,)), ((), ())), preferred_element_type=F32)


def legendre_kernel(leg, coef, out, legv, coefv, resv, lsem, csem, osem):
    def coef_copy(m):
        return pltpu.make_async_copy(coef.at[m], coefv.at[m], csem.at[m])

    for m in range(NM):
        for k in range(KT):
            pltpu.make_async_copy(leg.at[m, :, k], legv.at[m, k], lsem.at[m]).start()
        coef_copy(m).start()
    for m in range(NM):
        pltpu.make_async_copy(legv.at[m], legv.at[m], lsem.at[m]).wait()
        coef_copy(m).wait()
        total = jnp.zeros((2 * NBLK, 2 * NS), F32)
        for k in range(KT // 2):
            pair = [legv.at[m, 2 * k + i].reshape(2 * NBLK, 128)[...] for i in range(2)]
            total += dot(jnp.concatenate(pair, axis=1), coefv[m, k * 256 : (k + 1) * 256, :])
        rounded = total.astype(BF)
        for c in range(2):
            resv.at[m, c].reshape(2 * NBLK, 128)[...] = rounded[:, c * 128 : (c + 1) * 128]
            pltpu.make_async_copy(resv.at[m, c], out.at[:, c, m], osem).start()
    pltpu.make_async_copy(resv, resv, osem).wait()


def legendre_sums(legendre, coefficients):
    view = legendre.reshape(NM, NBLK, 2, KT, 128).transpose(0, 1, 3, 2, 4)
    return pl.pallas_call(
        legendre_kernel,
        out_shape=jax.ShapeDtypeStruct((NBLK, 2, NM, 2, 128), BF),
        in_specs=[anywhere(), anywhere()],
        out_specs=anywhere(),
        scratch_shapes=[
            pltpu.VMEM((NM, KT, NBLK, 2, 128), BF),
            pltpu.VMEM((NM, L, 2 * NS), BF),
            pltpu.VMEM((NM, 2, NBLK, 2, 128), BF),
            pltpu.SemaphoreType.DMA((NM,)),
            pltpu.SemaphoreType.DMA((NM,)),
            pltpu.SemaphoreType.DMA,
        ],
        compiler_params=params(60),
        cost_estimate=pl.CostEstimate(flops=2 * NM * 128 * L * 256, bytes_accessed=6 * MB, transcendentals=0),
        name="legendre_sums",
    )(view, coefficients)


def prepare_kernel(reg, holes, observed, boundary, orders, pb, ph, obsb, grp, lan, obsm, amat, bmat, pcol, rcol, rows):
    me = reg[0]
    h = holes[...].reshape(NG, 128)
    obs = observed[...].reshape(NG, 128)
    obsm[...] = jnp.where(h >= 0, 0.0, obs).astype(BF)

    hi, lo = h >> 4, h & 15
    a_iota, b_iota, lane = iota((32, 128), 0), iota((16, 128), 0), iota((32, 128), 1).astype(F32)
    for g in range(NG):
        hit = a_iota == hi[g : g + 1, :]
        at = pl.ds(g * 128, 128)
        amat[0:32, at] = jnp.where(hit, float(g + 1), 0.0).astype(BF)
        amat[32:64, at] = jnp.where(hit, lane, 0.0).astype(BF)
        bmat[:, at] = jnp.where(b_iota == lo[g : g + 1, :], 1.0, 0.0).astype(BF)
    tall = dot_nt(amat[...], bmat[...]).astype(BF)
    wide = dot_nt(bmat[...], amat[...]).astype(BF)
    pick = (iota((HMAX, 32), 0) // 16 == iota((HMAX, 32), 1)).astype(F32).astype(BF)
    low = iota((HMAX, 16), 0) % 16 == iota((HMAX, 16), 1)
    g1 = jnp.sum(jnp.where(low, dot(pick, tall[0:32]), 0.0), axis=1, keepdims=True)
    lh = jnp.sum(jnp.where(low, dot(pick, tall[32:64]), 0.0), axis=1, keepdims=True)
    pick_t = (iota((32, HMAX), 1) // 16 == iota((32, HMAX), 0)).astype(F32).astype(BF)
    low_t = iota((16, HMAX), 1) % 16 == iota((16, HMAX), 0)
    g1_row = jnp.sum(jnp.where(low_t, dot(wide[:, 0:32], pick_t), 0.0), axis=0, keepdims=True)
    grp[...] = jnp.where(iota((NT, HMAX), 0).astype(F32) == jnp.floor((g1_row - 1.0) * 0.5), 1.0, 0.0).astype(BF)
    gh = g1 - 1.0
    tile_h = jnp.floor(gh * 0.5)
    place = (gh - 2.0 * tile_h) * 128.0 + lh
    lan[...] = jnp.where(iota((HMAX, 256), 1).astype(F32) == place, 1.0, 0.0).astype(BF)
    pcol[NB:, :] = jnp.broadcast_to(tile_h * 128.0 + lh, (HMAX, 128))
    rcol[NB:, :] = jnp.broadcast_to(gh - 2.0 * tile_h, (HMAX, 128))

    mine = iota((SLOTS, NB), 1) == iota((SLOTS, NB), 0) + me * SLOTS
    cols = []
    for d in range(NREG):
        line = boundary[pl.ds(lax.rem(me + d, NREG), 1), :].astype(F32)
        cols.append(jnp.sum(jnp.where(mine, line, 0.0), axis=1, keepdims=True))
    u = jnp.concatenate(cols, axis=0) - (me * (2 * NPHI)).astype(F32)
    rb = jnp.where(u >= float(NPHI), 1.0, 0.0)
    p = u - rb * float(NPHI)
    tile_b = jnp.floor(p * (1.0 / 128.0))
    lane_b = p - tile_b * 128.0
    pcol[0:NB, :] = jnp.broadcast_to(p, (NB, 128))
    rcol[0:NB, :] = jnp.broadcast_to(rb, (NB, 128))
    one = jnp.where(iota((NB, NG), 1).astype(F32) == 2.0 * tile_b + rb, 1.0, 0.0).astype(BF)
    first = obs.astype(BF)
    rest = obs - first.astype(F32)
    second = rest.astype(BF)
    third = (rest - second.astype(F32)).astype(BF)
    value = dot(one, first) + dot(one, second) + dot(one, third)
    value = jnp.where(iota((NB, 128), 1).astype(F32) == lane_b, value, 0.0)
    obsb[...] = jnp.broadcast_to(jnp.sum(value, axis=1, keepdims=True), (NB, 128))

    line = jnp.broadcast_to(orders[...], (8, 256))
    split = jnp.concatenate([(line >> 3).astype(F32), (line & 7).astype(F32)], axis=0).astype(BF)
    at = iota((256, NK), 1)
    spread = (iota((256, NK), 0) == (at >> 4) * 4 + ((at & 7) >> 1)).astype(F32).astype(BF)
    both = dot(split, spread)
    order = both[0:8] * 8.0 + both[8:16]
    at = iota((8, NK), 1)
    rows[0] = order * (1.0 / NPHI)
    rows[1] = ((at >> 3) & 1).astype(F32) * 0.25
    rows[2] = (at & 1).astype(F32)
    rows[3] = jnp.where(order == 0.0, 1.0, 2.0)

    def phases(out, base):
        def step(i, _):
            at = pl.multiple_of(i * 16, 16)
            pc = pcol[pl.ds(base + at, 16), :]
            rc = rcol[pl.ds(base + at, 16), :]
            for t in range(NK // 128):
                ls = slice(t * 128, (t + 1) * 128)
                turn = pc * rows[0, 0:1, ls] + rows[1, 0:1, ls]
                turn = turn - ((turn + ROUND) - ROUND)
                z = turn * turn
                value = jnp.full((16, 128), COS[-1], F32)
                for c in COS[-2::-1]:
                    value = value * z + c
                weight = jnp.where(rc == rows[2, 0:1, ls], rows[3, 0:1, ls], 0.0)
                out[pl.ds(at, 16), ls] = (value * weight).astype(BF)
            return 0

        lax.fori_loop(0, out.shape[0] // 16, step, 0)

    phases(pb, 0)
    phases(ph, NB)


def prepare(reg, holes, observed, boundary, orders):
    shapes = [
        ((NB, NK), BF),
        ((HMAX, NK), BF),
        ((NB, 128), F32),
        ((NT, HMAX), BF),
        ((HMAX, 256), BF),
        ((NG, 128), BF),
    ]
    return pl.pallas_call(
        prepare_kernel,
        out_shape=[jax.ShapeDtypeStruct(s, t) for s, t in shapes],
        in_specs=[smem()] + [vmem()] * 4,
        out_specs=[vmem()] * 6,
        scratch_shapes=[
            pltpu.VMEM((64, 2 * NPHI), BF),
            pltpu.VMEM((16, 2 * NPHI), BF),
            pltpu.VMEM((NB + HMAX, 128), F32),
            pltpu.VMEM((NB + HMAX, 128), F32),
            pltpu.VMEM((4, 8, NK), F32),
        ],
        compiler_params=params(30),
        cost_estimate=pl.CostEstimate(flops=20_000_000, bytes_accessed=8 * MB, transcendentals=0),
        name="prepare",
    )(reg, holes, observed, boundary, orders)


def residual_kernel(spectra, pb, obsb, own, to1, to2, to3):
    sky = dot(pb[...], spectra[...]).astype(BF).astype(F32)
    residual = (obsb[...] - sky).astype(BF)
    for d, ref in enumerate((own, to1, to2, to3)):
        ref[...] = residual[d * SLOTS : (d + 1) * SLOTS, :]


def residuals(spectra, pb, obsb):
    return pl.pallas_call(
        residual_kernel,
        out_shape=[jax.ShapeDtypeStruct((SLOTS, NS), BF)] * NREG,
        in_specs=[vmem()] * 3,
        out_specs=[vmem()] * NREG,
        compiler_params=params(30),
        cost_estimate=pl.CostEstimate(flops=2 * NB * NK * NS, bytes_accessed=MB, transcendentals=0),
        name="residuals",
    )(spectra, pb, obsb)


def hole_kernel(reg, owners, spectra, ph, tile0, tile1, tile2, tile3, after, sky, tile):
    del after
    sky[...] = dot(ph[...], spectra[...]).astype(BF)
    me = reg[0]
    away = lax.rem(me - owners[0, me] + NREG, NREG)
    for d, ref in enumerate((tile0, tile1, tile2, tile3)):

        @pl.when(away == d)
        def _(ref=ref):
            tile[...] = ref[...]


def hole_sky(reg, owners, spectra, ph, tiles, after):
    return pl.pallas_call(
        hole_kernel,
        out_shape=[jax.ShapeDtypeStruct((HMAX, NS), BF), jax.ShapeDtypeStruct((HMAX, NB), BF)],
        in_specs=[smem(), smem()] + [vmem()] * 6 + [anywhere()],
        out_specs=[vmem()] * 2,
        compiler_params=params(30),
        cost_estimate=pl.CostEstimate(flops=2 * HMAX * NK * NS, bytes_accessed=2 * MB, transcendentals=0),
        name="hole_sky",
    )(reg, owners, spectra, ph, *tiles, after)


CHUNK = 8


def fill_kernel(reg, own, from1, from2, from3, tile, sky, grp, lan, obsm, out, edge, xt, outv, sem):
    me = reg[0]
    for d, ref in enumerate((own, from1, from2, from3)):
        source = lax.rem(me - d + NREG, NREG)
        edge[pl.ds(pl.multiple_of(source * SLOTS, SLOTS), SLOTS), :] = ref[...]
    correction = dot(tile[...], edge[...]).astype(BF)
    holes = (sky[...].astype(F32) + correction.astype(F32)).astype(BF).astype(F32)
    xt[...] = holes.T
    groups = grp[...]
    lanes = lan[...]
    base = obsm[...]

    def copy(i):
        at = pl.ds(i * CHUNK * NG, CHUNK * NG)
        return pltpu.make_async_copy(outv.at[at], out.at[at], sem)

    for i in range(NS // CHUNK):
        parts = [groups * xt[i * CHUNK + j : i * CHUNK + j + 1, :].astype(BF) for j in range(CHUNK)]
        got = dot(jnp.concatenate(parts, axis=0), lanes)
        got = got.reshape(CHUNK * NG, 128).astype(BF)
        for j in range(CHUNK):
            at = i * CHUNK * NG + j * NG
            outv[at : at + NG, :] = got[j * NG : (j + 1) * NG, :] + base
        copy(i).start()
    pltpu.make_async_copy(outv, outv, sem).wait()


def fill(reg, edges, tile, sky, grp, lan, obsm):
    return pl.pallas_call(
        fill_kernel,
        out_shape=jax.ShapeDtypeStruct((NS * NG, 128), BF),
        in_specs=[smem()] + [vmem()] * 9,
        out_specs=anywhere(),
        scratch_shapes=[
            pltpu.VMEM((NB, NS), BF),
            pltpu.VMEM((NS, HMAX), F32),
            pltpu.VMEM((NS * NG, 128), BF),
            pltpu.SemaphoreType.DMA,
        ],
        compiler_params=params(16),
        cost_estimate=pl.CostEstimate(flops=2 * NS * NG * HMAX * 128, bytes_accessed=3 * MB, transcendentals=0),
        name="fill",
    )(reg, *edges, tile, sky, grp, lan, obsm)


def by_lane_tile(x):
    return x.reshape(2, NPHI // 128, 128).transpose(1, 0, 2)


def shifted(x, d):
    return lax.ppermute(x, "reg", [(i, (i + d) % NREG) for i in range(NREG)])


def body(coefficients, legendre, harmonic_orders, observed, hole_rows, boundary, tile_owner, kriging):
    reg = lax.axis_index("reg").astype(I32).reshape(1)
    sums = legendre_sums(legendre, coefficients)
    spectra = lax.all_to_all(sums, "blk", split_axis=0, concat_axis=0, tiled=True).reshape(NK, 128)
    pb, ph, obsb, grp, lan, obsm = prepare(
        reg, by_lane_tile(hole_rows), by_lane_tile(observed), boundary.reshape(NREG, NB), harmonic_orders.reshape(1, -1)
    )
    tile = kriging.reshape(HMAX, NB)
    tiles = [tile] + [shifted(tile, d) for d in (1, 2, 3)]
    own, *away = residuals(spectra, pb, obsb)
    edges = [own] + [shifted(x, d + 1) for d, x in enumerate(away)]
    sky, my_tile = hole_sky(reg, tile_owner, spectra, ph, tiles, own)
    out = fill(reg, edges, my_tile, sky, grp, lan, obsm)
    return out.reshape(NS, NPHI // 128, 2, 128).transpose(0, 2, 1, 3).reshape(NS, 2, NPHI)


def solution(mesh):
    return jax.shard_map(
        body,
        mesh=mesh,
        in_specs=(
            P("blk", None, None),
            P("blk", None, "reg", None, None),
            P(),
            P(("blk", "reg"), None),
            P(("blk", "reg"), None),
            P("blk", None, None),
            P("blk", None),
            P("blk", "reg", None, None),
        ),
        out_specs=P(None, ("blk", "reg"), None),
        check_vma=False,
    )
```

```python
import functools

import jax
import jax.numpy as jnp
from jax import lax
from jax.experimental import pallas as pl
from jax.experimental.pallas import tpu as pltpu
from jax.sharding import PartitionSpec as P

BF = jnp.bfloat16
F32 = jnp.float32
I32 = jnp.int32
NBLK = 64
NREG = 4
NM = 4
L = 2048
KT = L // 128
NPHI = 4096
NT = NPHI // 128
NG = 2 * NT
NB = 256
SLOTS = NB // NREG
HMAX = 512
NS = 128
NK = NBLK * 16
MB = 1024 * 1024
ROUND = 12582912.0
COS = (
    0.9999999890590234,
    -19.739204499453898,
    64.93911745989367,
    -85.45013953084099,
    60.16763095056212,
    -25.967599246900118,
    6.528658158989,
)


def vmem():
    return pl.BlockSpec(memory_space=pltpu.VMEM)


def smem():
    return pl.BlockSpec(memory_space=pltpu.SMEM)


def anywhere():
    return pl.BlockSpec(memory_space=pl.ANY)


def params(mib):
    return pltpu.CompilerParams(vmem_limit_bytes=mib * MB)


def iota(shape, axis):
    return lax.broadcasted_iota(I32, shape, axis)


def dot(a, b):
    return jnp.dot(a, b, preferred_element_type=F32)


def dot_nt(a, b):
    return lax.dot_general(a, b, (((1,), (1,)), ((), ())), preferred_element_type=F32)


STEPS = 8
WIDE = KT // STEPS
DEEP = L // STEPS


def legendre_kernel(leg, coef, out, legv, coefv, lsem, csem):
    def coef_copy(k):
        at = pl.ds(k * DEEP, DEEP)
        return pltpu.make_async_copy(coef.at[:, at], coefv.at[:, at], csem.at[k])

    for k in range(STEPS):
        for t in range(k * WIDE, (k + 1) * WIDE):
            pltpu.make_async_copy(leg.at[:, :, t], legv.at[t], lsem.at[k]).start()
        coef_copy(k).start()
    totals = [jnp.zeros((2 * NBLK, 2 * NS), F32)] * NM
    for k in range(STEPS):
        part = legv.at[k * WIDE : (k + 1) * WIDE]
        pltpu.make_async_copy(part, part, lsem.at[k]).wait()
        coef_copy(k).wait()
        for m in range(NM):
            left = [legv.at[t, m].reshape(2 * NBLK, 128)[...] for t in range(k * WIDE, (k + 1) * WIDE)]
            totals[m] += dot(jnp.concatenate(left, axis=1), coefv[m, k * DEEP : (k + 1) * DEEP, :])
    for m in range(NM):
        rounded = totals[m].astype(BF)
        for c in range(2):
            out[:, c, m] = rounded[:, c * 128 : (c + 1) * 128].reshape(NBLK, 2, 128)


def legendre_sums(legendre, coefficients):
    view = legendre.reshape(NM, NBLK, 2, KT, 128).transpose(0, 1, 3, 2, 4)
    return pl.pallas_call(
        legendre_kernel,
        out_shape=jax.ShapeDtypeStruct((NBLK, 2, NM, 2, 128), BF),
        in_specs=[anywhere(), anywhere()],
        out_specs=vmem(),
        scratch_shapes=[
            pltpu.VMEM((KT, NM, NBLK, 2, 128), BF),
            pltpu.VMEM((NM, L, 2 * NS), BF),
            pltpu.SemaphoreType.DMA((STEPS,)),
            pltpu.SemaphoreType.DMA((STEPS,)),
        ],
        compiler_params=params(62),
        cost_estimate=pl.CostEstimate(flops=2 * NM * 128 * L * 256, bytes_accessed=6 * MB, transcendentals=0),
        name="legendre_sums",
    )(view, coefficients)


def prepare_kernel(reg, holes, observed, boundary, orders, pb, ph, obsb, grp, lan, obsm, amat, bmat, pcol, rcol, rows):
    me = reg[0]
    h = holes[...].reshape(NG, 128)
    obs = observed[...].reshape(NG, 128)
    obsm[...] = jnp.where(h >= 0, 0.0, obs).astype(BF)

    hi, lo = h >> 4, h & 15
    a_iota, b_iota, lane = iota((32, 128), 0), iota((16, 128), 0), iota((32, 128), 1).astype(F32)
    for g in range(NG):
        hit = a_iota == hi[g : g + 1, :]
        at = pl.ds(g * 128, 128)
        amat[0:32, at] = jnp.where(hit, float(g + 1), 0.0).astype(BF)
        amat[32:64, at] = jnp.where(hit, lane, 0.0).astype(BF)
        bmat[:, at] = jnp.where(b_iota == lo[g : g + 1, :], 1.0, 0.0).astype(BF)
    tall = dot_nt(amat[...], bmat[...]).astype(BF)
    wide = dot_nt(bmat[...], amat[...]).astype(BF)
    pick = (iota((HMAX, 32), 0) // 16 == iota((HMAX, 32), 1)).astype(F32).astype(BF)
    low = iota((HMAX, 16), 0) % 16 == iota((HMAX, 16), 1)
    g1 = jnp.sum(jnp.where(low, dot(pick, tall[0:32]), 0.0), axis=1, keepdims=True)
    lh = jnp.sum(jnp.where(low, dot(pick, tall[32:64]), 0.0), axis=1, keepdims=True)
    pick_t = (iota((32, HMAX), 1) // 16 == iota((32, HMAX), 0)).astype(F32).astype(BF)
    low_t = iota((16, HMAX), 1) % 16 == iota((16, HMAX), 0)
    g1_row = jnp.sum(jnp.where(low_t, dot(wide[:, 0:32], pick_t), 0.0), axis=0, keepdims=True)
    grp[...] = jnp.where(iota((NT, HMAX), 0).astype(F32) == jnp.floor((g1_row - 1.0) * 0.5), 1.0, 0.0).astype(BF)
    gh = g1 - 1.0
    tile_h = jnp.floor(gh * 0.5)
    place = (gh - 2.0 * tile_h) * 128.0 + lh
    lan[...] = jnp.where(iota((HMAX, 256), 1).astype(F32) == place, 1.0, 0.0).astype(BF)
    pcol[NB:, :] = jnp.broadcast_to(tile_h * 128.0 + lh, (HMAX, 128))
    rcol[NB:, :] = jnp.broadcast_to(gh - 2.0 * tile_h, (HMAX, 128))

    mine = iota((SLOTS, NB), 1) == iota((SLOTS, NB), 0) + me * SLOTS
    cols = []
    for d in range(NREG):
        line = boundary[pl.ds(lax.rem(me + d, NREG), 1), :].astype(F32)
        cols.append(jnp.sum(jnp.where(mine, line, 0.0), axis=1, keepdims=True))
    u = jnp.concatenate(cols, axis=0) - (me * (2 * NPHI)).astype(F32)
    rb = jnp.where(u >= float(NPHI), 1.0, 0.0)
    p = u - rb * float(NPHI)
    tile_b = jnp.floor(p * (1.0 / 128.0))
    lane_b = p - tile_b * 128.0
    pcol[0:NB, :] = jnp.broadcast_to(p, (NB, 128))
    rcol[0:NB, :] = jnp.broadcast_to(rb, (NB, 128))
    one = jnp.where(iota((NB, NG), 1).astype(F32) == 2.0 * tile_b + rb, 1.0, 0.0).astype(BF)
    first = obs.astype(BF)
    rest = obs - first.astype(F32)
    second = rest.astype(BF)
    third = (rest - second.astype(F32)).astype(BF)
    value = dot(one, first) + dot(one, second) + dot(one, third)
    value = jnp.where(iota((NB, 128), 1).astype(F32) == lane_b, value, 0.0)
    obsb[...] = jnp.broadcast_to(jnp.sum(value, axis=1, keepdims=True), (NB, 128))

    line = jnp.broadcast_to(orders[...], (8, 256))
    split = jnp.concatenate([(line >> 3).astype(F32), (line & 7).astype(F32)], axis=0).astype(BF)
    at = iota((256, NK), 1)
    spread = (iota((256, NK), 0) == (at >> 4) * 4 + ((at & 7) >> 1)).astype(F32).astype(BF)
    both = dot(split, spread)
    order = both[0:8] * 8.0 + both[8:16]
    at = iota((8, NK), 1)
    rows[0] = order * (1.0 / NPHI)
    rows[1] = ((at >> 3) & 1).astype(F32) * 0.25
    rows[2] = (at & 1).astype(F32)
    rows[3] = jnp.where(order == 0.0, 1.0, 2.0)

    def phases(out, base):
        def step(i, _):
            at = pl.multiple_of(i * 16, 16)
            pc = pcol[pl.ds(base + at, 16), :]
            rc = rcol[pl.ds(base + at, 16), :]
            for t in range(NK // 128):
                ls = slice(t * 128, (t + 1) * 128)
                turn = pc * rows[0, 0:1, ls] + rows[1, 0:1, ls]
                turn = turn - ((turn + ROUND) - ROUND)
                z = turn * turn
                value = jnp.full((16, 128), COS[-1], F32)
                for c in COS[-2::-1]:
                    value = value * z + c
                weight = jnp.where(rc == rows[2, 0:1, ls], rows[3, 0:1, ls], 0.0)
                out[pl.ds(at, 16), ls] = (value * weight).astype(BF)
            return 0

        lax.fori_loop(0, out.shape[0] // 16, step, 0)

    phases(pb, 0)
    phases(ph, NB)


def prepare(reg, holes, observed, boundary, orders):
    shapes = [
        ((NB, NK), BF),
        ((HMAX, NK), BF),
        ((NB, 128), F32),
        ((NT, HMAX), BF),
        ((HMAX, 256), BF),
        ((NG, 128), BF),
    ]
    return pl.pallas_call(
        prepare_kernel,
        out_shape=[jax.ShapeDtypeStruct(s, t) for s, t in shapes],
        in_specs=[smem()] + [vmem()] * 4,
        out_specs=[vmem()] * 6,
        scratch_shapes=[
            pltpu.VMEM((64, 2 * NPHI), BF),
            pltpu.VMEM((16, 2 * NPHI), BF),
            pltpu.VMEM((NB + HMAX, 128), F32),
            pltpu.VMEM((NB + HMAX, 128), F32),
            pltpu.VMEM((4, 8, NK), F32),
        ],
        compiler_params=params(30),
        cost_estimate=pl.CostEstimate(flops=20_000_000, bytes_accessed=8 * MB, transcendentals=0),
        name="prepare",
    )(reg, holes, observed, boundary, orders)


def residual_kernel(spectra, pb, obsb, own, to1, to2, to3):
    sky = dot(pb[...], spectra[...]).astype(BF).astype(F32)
    residual = (obsb[...] - sky).astype(BF)
    for d, ref in enumerate((own, to1, to2, to3)):
        ref[...] = residual[d * SLOTS : (d + 1) * SLOTS, :]


def residuals(spectra, pb, obsb):
    return pl.pallas_call(
        residual_kernel,
        out_shape=[jax.ShapeDtypeStruct((SLOTS, NS), BF)] * NREG,
        in_specs=[vmem()] * 3,
        out_specs=[vmem()] * NREG,
        compiler_params=params(30),
        cost_estimate=pl.CostEstimate(flops=2 * NB * NK * NS, bytes_accessed=MB, transcendentals=0),
        name="residuals",
    )(spectra, pb, obsb)


def hole_kernel(reg, owners, spectra, ph, tile0, tile1, tile2, tile3, after, sky, tile):
    del after
    sky[...] = dot(ph[...], spectra[...]).astype(BF)
    me = reg[0]
    away = lax.rem(me - owners[0, me] + NREG, NREG)
    for d, ref in enumerate((tile0, tile1, tile2, tile3)):

        @pl.when(away == d)
        def _(ref=ref):
            tile[...] = ref[...]


def hole_sky(reg, owners, spectra, ph, tiles, after):
    return pl.pallas_call(
        hole_kernel,
        out_shape=[jax.ShapeDtypeStruct((HMAX, NS), BF), jax.ShapeDtypeStruct((HMAX, NB), BF)],
        in_specs=[smem(), smem()] + [vmem()] * 6 + [anywhere()],
        out_specs=[vmem()] * 2,
        compiler_params=params(30),
        cost_estimate=pl.CostEstimate(flops=2 * HMAX * NK * NS, bytes_accessed=2 * MB, transcendentals=0),
        name="hole_sky",
    )(reg, owners, spectra, ph, *tiles, after)


CHUNK = 8


def fill_kernel(reg, own, from1, from2, from3, tile, sky, grp, lan, obsm, out, edge, xt, outv, sem):
    me = reg[0]
    for d, ref in enumerate((own, from1, from2, from3)):
        source = lax.rem(me - d + NREG, NREG)
        edge[pl.ds(pl.multiple_of(source * SLOTS, SLOTS), SLOTS), :] = ref[...]
    correction = dot(tile[...], edge[...]).astype(BF)
    holes = (sky[...].astype(F32) + correction.astype(F32)).astype(BF).astype(F32)
    xt[...] = holes.T
    groups = grp[...]
    lanes = lan[...]
    base = obsm[...].astype(F32)

    def copy(i):
        at = pl.ds(i * CHUNK * NG, CHUNK * NG)
        return pltpu.make_async_copy(outv.at[at], out.at[at], sem)

    for i in range(NS // CHUNK):
        parts = [groups * xt[i * CHUNK + j : i * CHUNK + j + 1, :].astype(BF) for j in range(CHUNK)]
        got = dot(jnp.concatenate(parts, axis=0), lanes)
        got = got.reshape(CHUNK * NG, 128)
        for j in range(CHUNK):
            at = i * CHUNK * NG + j * NG
            outv[at : at + NG, :] = (got[j * NG : (j + 1) * NG, :] + base).astype(BF)
        copy(i).start()
    pltpu.make_async_copy(outv, outv, sem).wait()


def fill(reg, edges, tile, sky, grp, lan, obsm):
    return pl.pallas_call(
        fill_kernel,
        out_shape=jax.ShapeDtypeStruct((NS * NG, 128), BF),
        in_specs=[smem()] + [vmem()] * 9,
        out_specs=anywhere(),
        scratch_shapes=[
            pltpu.VMEM((NB, NS), BF),
            pltpu.VMEM((NS, HMAX), F32),
            pltpu.VMEM((NS * NG, 128), BF),
            pltpu.SemaphoreType.DMA,
        ],
        compiler_params=params(16),
        cost_estimate=pl.CostEstimate(flops=2 * NS * NG * HMAX * 128, bytes_accessed=3 * MB, transcendentals=0),
        name="fill",
    )(reg, *edges, tile, sky, grp, lan, obsm)


def by_lane_tile(x):
    return x.reshape(2, NPHI // 128, 128).transpose(1, 0, 2)


def shifted(x, d):
    return lax.ppermute(x, "reg", [(i, (i + d) % NREG) for i in range(NREG)])


def body(coefficients, legendre, harmonic_orders, observed, hole_rows, boundary, tile_owner, kriging):
    reg = lax.axis_index("reg").astype(I32).reshape(1)
    sums = legendre_sums(legendre, coefficients)
    spectra = lax.all_to_all(sums, "blk", split_axis=0, concat_axis=0, tiled=True).reshape(NK, 128)
    pb, ph, obsb, grp, lan, obsm = prepare(
        reg, by_lane_tile(hole_rows), by_lane_tile(observed), boundary.reshape(NREG, NB), harmonic_orders.reshape(1, -1)
    )
    tile = kriging.reshape(HMAX, NB)
    tiles = [tile] + [shifted(tile, d) for d in (1, 2, 3)]
    own, *away = residuals(spectra, pb, obsb)
    edges = [own] + [shifted(x, d + 1) for d, x in enumerate(away)]
    sky, my_tile = hole_sky(reg, tile_owner, spectra, ph, tiles, own)
    out = fill(reg, edges, my_tile, sky, grp, lan, obsm)
    return out.reshape(NS, NPHI // 128, 2, 128).transpose(0, 2, 1, 3).reshape(NS, 2, NPHI)


def solution(mesh):
    return jax.shard_map(
        body,
        mesh=mesh,
        in_specs=(
            P("blk", None, None),
            P("blk", None, "reg", None, None),
            P(),
            P(("blk", "reg"), None),
            P(("blk", "reg"), None),
            P("blk", None, None),
            P("blk", None),
            P("blk", "reg", None, None),
        ),
        out_specs=P(None, ("blk", "reg"), None),
        check_vma=False,
    )
```

```python
import functools

import jax
import jax.numpy as jnp
from jax import lax
from jax.experimental import pallas as pl
from jax.experimental.pallas import tpu as pltpu
from jax.sharding import PartitionSpec as P

BF = jnp.bfloat16
F32 = jnp.float32
I32 = jnp.int32
NBLK = 64
NREG = 4
NM = 4
L = 2048
KT = L // 128
NPHI = 4096
NT = NPHI // 128
NG = 2 * NT
NB = 256
SLOTS = NB // NREG
HMAX = 512
NS = 128
NK = NBLK * 16
MB = 1024 * 1024
ROUND = 12582912.0
COS = (
    0.9999999890590234,
    -19.739204499453898,
    64.93911745989367,
    -85.45013953084099,
    60.16763095056212,
    -25.967599246900118,
    6.528658158989,
)


def vmem():
    return pl.BlockSpec(memory_space=pltpu.VMEM)


def smem():
    return pl.BlockSpec(memory_space=pltpu.SMEM)


def anywhere():
    return pl.BlockSpec(memory_space=pl.ANY)


def params(mib):
    return pltpu.CompilerParams(vmem_limit_bytes=mib * MB)


def iota(shape, axis):
    return lax.broadcasted_iota(I32, shape, axis)


def dot(a, b):
    return jnp.dot(a, b, preferred_element_type=F32)


def dot_nt(a, b):
    return lax.dot_general(a, b, (((1,), (1,)), ((), ())), preferred_element_type=F32)


STEPS = 8
WIDE = KT // STEPS
DEEP = L // STEPS


def legendre_kernel(leg, coef, out, legv, coefv, lsem, csem):
    def coef_copy(k):
        at = pl.ds(k * DEEP, DEEP)
        return pltpu.make_async_copy(coef.at[:, at], coefv.at[:, at], csem.at[k])

    for k in range(STEPS):
        for t in range(k * WIDE, (k + 1) * WIDE):
            pltpu.make_async_copy(leg.at[:, :, t], legv.at[t], lsem.at[k]).start()
        coef_copy(k).start()
    totals = [jnp.zeros((2 * NBLK, 2 * NS), F32)] * NM
    for k in range(STEPS):
        part = legv.at[k * WIDE : (k + 1) * WIDE]
        pltpu.make_async_copy(part, part, lsem.at[k]).wait()
        coef_copy(k).wait()
        for m in range(NM):
            left = [legv.at[t, m].reshape(2 * NBLK, 128)[...] for t in range(k * WIDE, (k + 1) * WIDE)]
            totals[m] += dot(jnp.concatenate(left, axis=1), coefv[m, k * DEEP : (k + 1) * DEEP, :])
    for m in range(NM):
        rounded = totals[m].astype(BF)
        for c in range(2):
            out[:, c, m] = rounded[:, c * 128 : (c + 1) * 128].reshape(NBLK, 2, 128)


def legendre_sums(legendre, coefficients):
    view = legendre.reshape(NM, NBLK, 2, KT, 128).transpose(0, 1, 3, 2, 4)
    return pl.pallas_call(
        legendre_kernel,
        out_shape=jax.ShapeDtypeStruct((NBLK, 2, NM, 2, 128), BF),
        in_specs=[anywhere(), anywhere()],
        out_specs=vmem(),
        scratch_shapes=[
            pltpu.VMEM((KT, NM, NBLK, 2, 128), BF),
            pltpu.VMEM((NM, L, 2 * NS), BF),
            pltpu.SemaphoreType.DMA((STEPS,)),
            pltpu.SemaphoreType.DMA((STEPS,)),
        ],
        compiler_params=params(62),
        cost_estimate=pl.CostEstimate(flops=2 * NM * 128 * L * 256, bytes_accessed=6 * MB, transcendentals=0),
        name="legendre_sums",
    )(view, coefficients)


def prepare_kernel(reg, holes, observed, boundary, orders, pb, ph, obsb, grp, lan, obsm, amat, bmat, pcol, rcol, rows):
    me = reg[0]
    h = holes[...].reshape(NG, 128)
    obs = observed[...].reshape(NG, 128)
    obsm[...] = jnp.where(h >= 0, 0.0, obs).astype(BF)

    hi, lo = h >> 4, h & 15
    a_iota, b_iota, lane = iota((32, 128), 0), iota((16, 128), 0), iota((32, 128), 1).astype(F32)
    for g in range(NG):
        hit = a_iota == hi[g : g + 1, :]
        at = pl.ds(g * 128, 128)
        amat[0:32, at] = jnp.where(hit, float(g + 1), 0.0).astype(BF)
        amat[32:64, at] = jnp.where(hit, lane, 0.0).astype(BF)
        bmat[:, at] = jnp.where(b_iota == lo[g : g + 1, :], 1.0, 0.0).astype(BF)
    tall = dot_nt(amat[...], bmat[...]).astype(BF)
    wide = dot_nt(bmat[...], amat[...]).astype(BF)
    pick = (iota((HMAX, 32), 0) // 16 == iota((HMAX, 32), 1)).astype(F32).astype(BF)
    low = iota((HMAX, 16), 0) % 16 == iota((HMAX, 16), 1)
    g1 = jnp.sum(jnp.where(low, dot(pick, tall[0:32]), 0.0), axis=1, keepdims=True)
    lh = jnp.sum(jnp.where(low, dot(pick, tall[32:64]), 0.0), axis=1, keepdims=True)
    pick_t = (iota((32, HMAX), 1) // 16 == iota((32, HMAX), 0)).astype(F32).astype(BF)
    low_t = iota((16, HMAX), 1) % 16 == iota((16, HMAX), 0)
    g1_row = jnp.sum(jnp.where(low_t, dot(wide[:, 0:32], pick_t), 0.0), axis=0, keepdims=True)
    grp[...] = jnp.where(iota((NT, HMAX), 0).astype(F32) == jnp.floor((g1_row - 1.0) * 0.5), 1.0, 0.0).astype(BF)
    gh = g1 - 1.0
    tile_h = jnp.floor(gh * 0.5)
    place = (gh - 2.0 * tile_h) * 128.0 + lh
    lan[...] = jnp.where(iota((HMAX, 256), 1).astype(F32) == place, 1.0, 0.0).astype(BF)
    pcol[NB:, :] = jnp.broadcast_to(tile_h * 128.0 + lh, (HMAX, 128))
    rcol[NB:, :] = jnp.broadcast_to(gh - 2.0 * tile_h, (HMAX, 128))

    mine = iota((SLOTS, NB), 1) == iota((SLOTS, NB), 0) + me * SLOTS
    cols = []
    for d in range(NREG):
        line = boundary[pl.ds(lax.rem(me + d, NREG), 1), :].astype(F32)
        cols.append(jnp.sum(jnp.where(mine, line, 0.0), axis=1, keepdims=True))
    u = jnp.concatenate(cols, axis=0) - (me * (2 * NPHI)).astype(F32)
    rb = jnp.where(u >= float(NPHI), 1.0, 0.0)
    p = u - rb * float(NPHI)
    tile_b = jnp.floor(p * (1.0 / 128.0))
    lane_b = p - tile_b * 128.0
    pcol[0:NB, :] = jnp.broadcast_to(p, (NB, 128))
    rcol[0:NB, :] = jnp.broadcast_to(rb, (NB, 128))
    one = jnp.where(iota((NB, NG), 1).astype(F32) == 2.0 * tile_b + rb, 1.0, 0.0).astype(BF)
    first = obs.astype(BF)
    rest = obs - first.astype(F32)
    second = rest.astype(BF)
    third = (rest - second.astype(F32)).astype(BF)
    value = dot(one, first) + dot(one, second) + dot(one, third)
    value = jnp.where(iota((NB, 128), 1).astype(F32) == lane_b, value, 0.0)
    obsb[...] = jnp.broadcast_to(jnp.sum(value, axis=1, keepdims=True), (NB, 128))

    line = jnp.broadcast_to(orders[...], (8, 256))
    split = jnp.concatenate([(line >> 3).astype(F32), (line & 7).astype(F32)], axis=0).astype(BF)
    at = iota((256, NK), 1)
    spread = (iota((256, NK), 0) == (at >> 4) * 4 + ((at & 7) >> 1)).astype(F32).astype(BF)
    both = dot(split, spread)
    order = both[0:8] * 8.0 + both[8:16]
    at = iota((8, NK), 1)
    rows[0] = order * (1.0 / NPHI)
    rows[1] = ((at >> 3) & 1).astype(F32) * 0.25
    rows[2] = (at & 1).astype(F32)
    rows[3] = jnp.where(order == 0.0, 1.0, 2.0)

    def phases(out, base):
        def step(i, _):
            at = pl.multiple_of(i * 16, 16)
            pc = pcol[pl.ds(base + at, 16), :]
            rc = rcol[pl.ds(base + at, 16), :]
            for t in range(NK // 128):
                ls = slice(t * 128, (t + 1) * 128)
                turn = pc * rows[0, 0:1, ls] + rows[1, 0:1, ls]
                turn = turn - ((turn + ROUND) - ROUND)
                z = turn * turn
                value = jnp.full((16, 128), COS[-1], F32)
                for c in COS[-2::-1]:
                    value = value * z + c
                weight = jnp.where(rc == rows[2, 0:1, ls], rows[3, 0:1, ls], 0.0)
                out[pl.ds(at, 16), ls] = (value * weight).astype(BF)
            return 0

        lax.fori_loop(0, out.shape[0] // 16, step, 0)

    phases(pb, 0)
    phases(ph, NB)


def prepare(reg, holes, observed, boundary, orders):
    shapes = [
        ((NB, NK), BF),
        ((HMAX, NK), BF),
        ((NB, 128), F32),
        ((NT, HMAX), BF),
        ((HMAX, 256), BF),
        ((NG, 128), BF),
    ]
    return pl.pallas_call(
        prepare_kernel,
        out_shape=[jax.ShapeDtypeStruct(s, t) for s, t in shapes],
        in_specs=[smem()] + [vmem()] * 4,
        out_specs=[vmem()] * 6,
        scratch_shapes=[
            pltpu.VMEM((64, 2 * NPHI), BF),
            pltpu.VMEM((16, 2 * NPHI), BF),
            pltpu.VMEM((NB + HMAX, 128), F32),
            pltpu.VMEM((NB + HMAX, 128), F32),
            pltpu.VMEM((4, 8, NK), F32),
        ],
        compiler_params=params(30),
        cost_estimate=pl.CostEstimate(flops=20_000_000, bytes_accessed=8 * MB, transcendentals=0),
        name="prepare",
    )(reg, holes, observed, boundary, orders)


def residual_kernel(spectra, pb, obsb, own, to1, to2, to3):
    sky = dot(pb[...], spectra[...]).astype(BF).astype(F32)
    residual = (obsb[...] - sky).astype(BF)
    for d, ref in enumerate((own, to1, to2, to3)):
        ref[...] = residual[d * SLOTS : (d + 1) * SLOTS, :]


def residuals(spectra, pb, obsb):
    return pl.pallas_call(
        residual_kernel,
        out_shape=[jax.ShapeDtypeStruct((SLOTS, NS), BF)] * NREG,
        in_specs=[vmem()] * 3,
        out_specs=[vmem()] * NREG,
        compiler_params=params(30),
        cost_estimate=pl.CostEstimate(flops=2 * NB * NK * NS, bytes_accessed=MB, transcendentals=0),
        name="residuals",
    )(spectra, pb, obsb)


def hole_kernel(reg, owners, spectra, ph, tile0, tile1, tile2, tile3, after, sky, tile):
    del after
    sky[...] = dot(ph[...], spectra[...]).T.astype(BF)
    me = reg[0]
    away = lax.rem(me - owners[0, me] + NREG, NREG)
    for d, ref in enumerate((tile0, tile1, tile2, tile3)):

        @pl.when(away == d)
        def _(ref=ref):
            tile[...] = ref[...].T


def hole_sky(reg, owners, spectra, ph, tiles, after):
    return pl.pallas_call(
        hole_kernel,
        out_shape=[jax.ShapeDtypeStruct((NS, HMAX), BF), jax.ShapeDtypeStruct((NB, HMAX), BF)],
        in_specs=[smem(), smem()] + [vmem()] * 6 + [anywhere()],
        out_specs=[vmem()] * 2,
        compiler_params=params(30),
        cost_estimate=pl.CostEstimate(flops=2 * HMAX * NK * NS, bytes_accessed=2 * MB, transcendentals=0),
        name="hole_sky",
    )(reg, owners, spectra, ph, *tiles, after)


CHUNK = 8


def fill_kernel(reg, own, from1, from2, from3, tile, sky, grp, lan, obsm, out, edge, xt, outv, sem):
    me = reg[0]
    for d, ref in enumerate((own, from1, from2, from3)):
        source = lax.rem(me - d + NREG, NREG)
        edge[pl.ds(pl.multiple_of(source * SLOTS, SLOTS), SLOTS), :] = ref[...]
    correction = dot(edge[...].T, tile[...]).astype(BF)
    xt[...] = (sky[...].astype(F32) + correction.astype(F32)).astype(BF).astype(F32)
    groups = grp[...]
    lanes = lan[...]
    base = obsm[...].astype(F32)

    def copy(i):
        at = pl.ds(i * CHUNK * NG, CHUNK * NG)
        return pltpu.make_async_copy(outv.at[at], out.at[at], sem)

    for i in range(NS // CHUNK):
        parts = [groups * xt[i * CHUNK + j : i * CHUNK + j + 1, :].astype(BF) for j in range(CHUNK)]
        got = dot(jnp.concatenate(parts, axis=0), lanes)
        got = got.reshape(CHUNK * NG, 128)
        for j in range(CHUNK):
            at = i * CHUNK * NG + j * NG
            outv[at : at + NG, :] = (got[j * NG : (j + 1) * NG, :] + base).astype(BF)
        copy(i).start()
    pltpu.make_async_copy(outv, outv, sem).wait()


def fill(reg, edges, tile, sky, grp, lan, obsm):
    return pl.pallas_call(
        fill_kernel,
        out_shape=jax.ShapeDtypeStruct((NS * NG, 128), BF),
        in_specs=[smem()] + [vmem()] * 9,
        out_specs=anywhere(),
        scratch_shapes=[
            pltpu.VMEM((NB, NS), BF),
            pltpu.VMEM((NS, HMAX), F32),
            pltpu.VMEM((NS * NG, 128), BF),
            pltpu.SemaphoreType.DMA,
        ],
        compiler_params=params(16),
        cost_estimate=pl.CostEstimate(flops=2 * NS * NG * HMAX * 128, bytes_accessed=3 * MB, transcendentals=0),
        name="fill",
    )(reg, *edges, tile, sky, grp, lan, obsm)


def by_lane_tile(x):
    return x.reshape(2, NPHI // 128, 128).transpose(1, 0, 2)


def shifted(x, d):
    return lax.ppermute(x, "reg", [(i, (i + d) % NREG) for i in range(NREG)])


def body(coefficients, legendre, harmonic_orders, observed, hole_rows, boundary, tile_owner, kriging):
    reg = lax.axis_index("reg").astype(I32).reshape(1)
    sums = legendre_sums(legendre, coefficients)
    spectra = lax.all_to_all(sums, "blk", split_axis=0, concat_axis=0, tiled=True).reshape(NK, 128)
    pb, ph, obsb, grp, lan, obsm = prepare(
        reg, by_lane_tile(hole_rows), by_lane_tile(observed), boundary.reshape(NREG, NB), harmonic_orders.reshape(1, -1)
    )
    tile = kriging.reshape(HMAX, NB)
    tiles = [tile] + [shifted(tile, d) for d in (1, 2, 3)]
    own, *away = residuals(spectra, pb, obsb)
    edges = [own] + [shifted(x, d + 1) for d, x in enumerate(away)]
    sky, my_tile = hole_sky(reg, tile_owner, spectra, ph, tiles, own)
    out = fill(reg, edges, my_tile, sky, grp, lan, obsm)
    return out.reshape(NS, NPHI // 128, 2, 128).transpose(0, 2, 1, 3).reshape(NS, 2, NPHI)


def solution(mesh):
    return jax.shard_map(
        body,
        mesh=mesh,
        in_specs=(
            P("blk", None, None),
            P("blk", None, "reg", None, None),
            P(),
            P(("blk", "reg"), None),
            P(("blk", "reg"), None),
            P("blk", None, None),
            P("blk", None),
            P("blk", "reg", None, None),
        ),
        out_specs=P(None, ("blk", "reg"), None),
        check_vma=False,
    )
```

```python
import functools

import jax
import jax.numpy as jnp
from jax import lax
from jax.experimental import pallas as pl
from jax.experimental.pallas import tpu as pltpu
from jax.sharding import PartitionSpec as P

BF = jnp.bfloat16
F32 = jnp.float32
I32 = jnp.int32
NBLK = 64
NREG = 4
NM = 4
L = 2048
KT = L // 128
NPHI = 4096
NT = NPHI // 128
NG = 2 * NT
NB = 256
SLOTS = NB // NREG
HMAX = 512
NS = 128
NK = NBLK * 16
MB = 1024 * 1024
ROUND = 12582912.0
COS = (
    0.9999999890590234,
    -19.739204499453898,
    64.93911745989367,
    -85.45013953084099,
    60.16763095056212,
    -25.967599246900118,
    6.528658158989,
)


def vmem():
    return pl.BlockSpec(memory_space=pltpu.VMEM)


def smem():
    return pl.BlockSpec(memory_space=pltpu.SMEM)


def anywhere():
    return pl.BlockSpec(memory_space=pl.ANY)


def params(mib):
    return pltpu.CompilerParams(vmem_limit_bytes=mib * MB)


def iota(shape, axis):
    return lax.broadcasted_iota(I32, shape, axis)


def dot(a, b):
    return jnp.dot(a, b, preferred_element_type=F32)


def dot_nt(a, b):
    return lax.dot_general(a, b, (((1,), (1,)), ((), ())), preferred_element_type=F32)


STEPS = 8
WIDE = KT // STEPS
DEEP = L // STEPS


def legendre_kernel(leg, coef, out, legv, coefv, lsem, csem):
    def coef_copy(k):
        at = pl.ds(k * DEEP, DEEP)
        return pltpu.make_async_copy(coef.at[:, at], coefv.at[:, at], csem.at[k])

    for k in range(STEPS):
        for t in range(k * WIDE, (k + 1) * WIDE):
            pltpu.make_async_copy(leg.at[:, :, t], legv.at[t], lsem.at[k]).start()
        coef_copy(k).start()
    totals = [jnp.zeros((2 * NBLK, 2 * NS), F32)] * NM
    for k in range(STEPS):
        part = legv.at[k * WIDE : (k + 1) * WIDE]
        pltpu.make_async_copy(part, part, lsem.at[k]).wait()
        coef_copy(k).wait()
        for m in range(NM):
            left = [legv.at[t, m].reshape(2 * NBLK, 128)[...] for t in range(k * WIDE, (k + 1) * WIDE)]
            totals[m] += dot(jnp.concatenate(left, axis=1), coefv[m, k * DEEP : (k + 1) * DEEP, :])
    for m in range(NM):
        rounded = totals[m].astype(BF)
        for c in range(2):
            out[:, c, m] = rounded[:, c * 128 : (c + 1) * 128].reshape(NBLK, 2, 128)


def legendre_sums(legendre, coefficients):
    view = legendre.reshape(NM, NBLK, 2, KT, 128).transpose(0, 1, 3, 2, 4)
    return pl.pallas_call(
        legendre_kernel,
        out_shape=jax.ShapeDtypeStruct((NBLK, 2, NM, 2, 128), BF),
        in_specs=[anywhere(), anywhere()],
        out_specs=vmem(),
        scratch_shapes=[
            pltpu.VMEM((KT, NM, NBLK, 2, 128), BF),
            pltpu.VMEM((NM, L, 2 * NS), BF),
            pltpu.SemaphoreType.DMA((STEPS,)),
            pltpu.SemaphoreType.DMA((STEPS,)),
        ],
        compiler_params=params(62),
        cost_estimate=pl.CostEstimate(flops=2 * NM * 128 * L * 256, bytes_accessed=6 * MB, transcendentals=0),
        name="legendre_sums",
    )(view, coefficients)


def prepare_kernel(reg, holes, observed, boundary, orders, pb, ph, obsb, grp, lan, obsm, amat, bmat, pcol, rcol, rows):
    me = reg[0]
    h = holes[...].reshape(NG, 128)
    obs = observed[...].reshape(NG, 128)
    obsm[...] = jnp.where(h >= 0, 0.0, obs).astype(BF)

    hi, lo = h >> 4, h & 15
    a_iota, b_iota, lane = iota((32, 128), 0), iota((16, 128), 0), iota((32, 128), 1).astype(F32)
    for g in range(NG):
        hit = a_iota == hi[g : g + 1, :]
        at = pl.ds(g * 128, 128)
        amat[0:32, at] = jnp.where(hit, float(g + 1), 0.0).astype(BF)
        amat[32:64, at] = jnp.where(hit, lane, 0.0).astype(BF)
        bmat[:, at] = jnp.where(b_iota == lo[g : g + 1, :], 1.0, 0.0).astype(BF)
    tall = dot_nt(amat[...], bmat[...]).astype(BF)
    wide = dot_nt(bmat[...], amat[...]).astype(BF)
    pick = (iota((HMAX, 32), 0) // 16 == iota((HMAX, 32), 1)).astype(F32).astype(BF)
    low = iota((HMAX, 16), 0) % 16 == iota((HMAX, 16), 1)
    g1 = jnp.sum(jnp.where(low, dot(pick, tall[0:32]), 0.0), axis=1, keepdims=True)
    lh = jnp.sum(jnp.where(low, dot(pick, tall[32:64]), 0.0), axis=1, keepdims=True)
    pick_t = (iota((32, HMAX), 1) // 16 == iota((32, HMAX), 0)).astype(F32).astype(BF)
    low_t = iota((16, HMAX), 1) % 16 == iota((16, HMAX), 0)
    g1_row = jnp.sum(jnp.where(low_t, dot(wide[:, 0:32], pick_t), 0.0), axis=0, keepdims=True)
    grp[...] = jnp.where(iota((NT, HMAX), 0).astype(F32) == jnp.floor((g1_row - 1.0) * 0.5), 1.0, 0.0).astype(BF)
    gh = g1 - 1.0
    tile_h = jnp.floor(gh * 0.5)
    place = (gh - 2.0 * tile_h) * 128.0 + lh
    lan[...] = jnp.where(iota((HMAX, 256), 1).astype(F32) == place, 1.0, 0.0).astype(BF)
    pcol[NB:, :] = jnp.broadcast_to(tile_h * 128.0 + lh, (HMAX, 128))
    rcol[NB:, :] = jnp.broadcast_to(gh - 2.0 * tile_h, (HMAX, 128))

    mine = iota((SLOTS, NB), 1) == iota((SLOTS, NB), 0) + me * SLOTS
    cols = []
    for d in range(NREG):
        line = boundary[pl.ds(lax.rem(me + d, NREG), 1), :].astype(F32)
        cols.append(jnp.sum(jnp.where(mine, line, 0.0), axis=1, keepdims=True))
    u = jnp.concatenate(cols, axis=0) - (me * (2 * NPHI)).astype(F32)
    rb = jnp.where(u >= float(NPHI), 1.0, 0.0)
    p = u - rb * float(NPHI)
    tile_b = jnp.floor(p * (1.0 / 128.0))
    lane_b = p - tile_b * 128.0
    pcol[0:NB, :] = jnp.broadcast_to(p, (NB, 128))
    rcol[0:NB, :] = jnp.broadcast_to(rb, (NB, 128))
    one = jnp.where(iota((NB, NG), 1).astype(F32) == 2.0 * tile_b + rb, 1.0, 0.0).astype(BF)
    first = obs.astype(BF)
    rest = obs - first.astype(F32)
    second = rest.astype(BF)
    third = (rest - second.astype(F32)).astype(BF)
    value = dot(one, first) + dot(one, second) + dot(one, third)
    value = jnp.where(iota((NB, 128), 1).astype(F32) == lane_b, value, 0.0)
    obsb[...] = jnp.broadcast_to(jnp.sum(value, axis=1, keepdims=True), (NB, 128))

    line = jnp.broadcast_to(orders[...], (8, 256))
    split = jnp.concatenate([(line >> 3).astype(F32), (line & 7).astype(F32)], axis=0).astype(BF)
    at = iota((256, NK), 1)
    spread = (iota((256, NK), 0) == (at >> 4) * 4 + ((at & 7) >> 1)).astype(F32).astype(BF)
    both = dot(split, spread)
    order = both[0:8] * 8.0 + both[8:16]
    at = iota((8, NK), 1)
    rows[0] = order * (1.0 / NPHI)
    rows[1] = ((at >> 3) & 1).astype(F32) * 0.25
    rows[2] = (at & 1).astype(F32)
    rows[3] = jnp.where(order == 0.0, 1.0, 2.0)

    def phases(out, base):
        def step(i, _):
            at = pl.multiple_of(i * 16, 16)
            pc = pcol[pl.ds(base + at, 16), :]
            rc = rcol[pl.ds(base + at, 16), :]
            for t in range(NK // 128):
                ls = slice(t * 128, (t + 1) * 128)
                turn = pc * rows[0, 0:1, ls] + rows[1, 0:1, ls]
                turn = turn - ((turn + ROUND) - ROUND)
                z = turn * turn
                value = jnp.full((16, 128), COS[-1], F32)
                for c in COS[-2::-1]:
                    value = value * z + c
                weight = jnp.where(rc == rows[2, 0:1, ls], rows[3, 0:1, ls], 0.0)
                out[pl.ds(at, 16), ls] = (value * weight).astype(BF)
            return 0

        lax.fori_loop(0, out.shape[0] // 16, step, 0)

    phases(pb, 0)
    phases(ph, NB)


def prepare(reg, holes, observed, boundary, orders):
    shapes = [
        ((NB, NK), BF),
        ((HMAX, NK), BF),
        ((NB, 128), F32),
        ((NT, HMAX), BF),
        ((HMAX, 256), BF),
        ((NG, 128), BF),
    ]
    return pl.pallas_call(
        prepare_kernel,
        out_shape=[jax.ShapeDtypeStruct(s, t) for s, t in shapes],
        in_specs=[smem()] + [vmem()] * 4,
        out_specs=[vmem()] * 6,
        scratch_shapes=[
            pltpu.VMEM((64, 2 * NPHI), BF),
            pltpu.VMEM((16, 2 * NPHI), BF),
            pltpu.VMEM((NB + HMAX, 128), F32),
            pltpu.VMEM((NB + HMAX, 128), F32),
            pltpu.VMEM((4, 8, NK), F32),
        ],
        compiler_params=params(30),
        cost_estimate=pl.CostEstimate(flops=20_000_000, bytes_accessed=8 * MB, transcendentals=0),
        name="prepare",
    )(reg, holes, observed, boundary, orders)


def residual_kernel(spectra, pb, obsb, *away):
    sky = dot(pb[SLOTS:], spectra[...]).astype(BF).astype(F32)
    residual = (obsb[SLOTS:] - sky).astype(BF)
    for d, ref in enumerate(away):
        ref[...] = residual[d * SLOTS : (d + 1) * SLOTS, :]


def residuals(spectra, pb, obsb):
    return pl.pallas_call(
        residual_kernel,
        out_shape=[jax.ShapeDtypeStruct((SLOTS, NS), BF)] * (NREG - 1),
        in_specs=[vmem()] * 3,
        out_specs=[vmem()] * (NREG - 1),
        compiler_params=params(30),
        cost_estimate=pl.CostEstimate(flops=2 * (NB - SLOTS) * NK * NS, bytes_accessed=MB, transcendentals=0),
        name="residuals",
    )(spectra, pb, obsb)


def hole_kernel(reg, owners, spectra, ph, pb, obsb, tile0, tile1, tile2, tile3, after, sky, tile, own):
    del after
    sky[...] = dot(ph[...], spectra[...]).T.astype(BF)
    edge = dot(pb[0:SLOTS], spectra[...]).astype(BF).astype(F32)
    own[...] = (obsb[0:SLOTS] - edge).astype(BF)
    me = reg[0]
    away = lax.rem(me - owners[0, me] + NREG, NREG)
    for d, ref in enumerate((tile0, tile1, tile2, tile3)):

        @pl.when(away == d)
        def _(ref=ref):
            tile[...] = ref[...].T


def hole_sky(reg, owners, spectra, ph, pb, obsb, tiles, after):
    return pl.pallas_call(
        hole_kernel,
        out_shape=[jax.ShapeDtypeStruct(s, BF) for s in ((NS, HMAX), (NB, HMAX), (SLOTS, NS))],
        in_specs=[smem(), smem()] + [vmem()] * 8 + [anywhere()],
        out_specs=[vmem()] * 3,
        compiler_params=params(30),
        cost_estimate=pl.CostEstimate(flops=2 * HMAX * NK * NS, bytes_accessed=2 * MB, transcendentals=0),
        name="hole_sky",
    )(reg, owners, spectra, ph, pb, obsb, *tiles, after)


CHUNK = 8


def fill_kernel(reg, own, from1, from2, from3, tile, sky, grp, lan, obsm, out, edge, xt, outv, sem):
    me = reg[0]
    for d, ref in enumerate((own, from1, from2, from3)):
        source = lax.rem(me - d + NREG, NREG)
        edge[pl.ds(pl.multiple_of(source * SLOTS, SLOTS), SLOTS), :] = ref[...]
    correction = dot(edge[...].T, tile[...]).astype(BF)
    xt[...] = (sky[...].astype(F32) + correction.astype(F32)).astype(BF).astype(F32)
    groups = grp[...]
    lanes = lan[...]
    base = obsm[...].astype(F32)

    def copy(i):
        at = pl.ds(i * CHUNK * NG, CHUNK * NG)
        return pltpu.make_async_copy(outv.at[at], out.at[at], sem)

    for i in range(NS // CHUNK):
        parts = [groups * xt[i * CHUNK + j : i * CHUNK + j + 1, :].astype(BF) for j in range(CHUNK)]
        got = dot(jnp.concatenate(parts, axis=0), lanes)
        got = got.reshape(CHUNK * NG, 128)
        for j in range(CHUNK):
            at = i * CHUNK * NG + j * NG
            outv[at : at + NG, :] = (got[j * NG : (j + 1) * NG, :] + base).astype(BF)
        copy(i).start()
    pltpu.make_async_copy(outv, outv, sem).wait()


def fill(reg, edges, tile, sky, grp, lan, obsm):
    return pl.pallas_call(
        fill_kernel,
        out_shape=jax.ShapeDtypeStruct((NS * NG, 128), BF),
        in_specs=[smem()] + [vmem()] * 9,
        out_specs=anywhere(),
        scratch_shapes=[
            pltpu.VMEM((NB, NS), BF),
            pltpu.VMEM((NS, HMAX), F32),
            pltpu.VMEM((NS * NG, 128), BF),
            pltpu.SemaphoreType.DMA,
        ],
        compiler_params=params(16),
        cost_estimate=pl.CostEstimate(flops=2 * NS * NG * HMAX * 128, bytes_accessed=3 * MB, transcendentals=0),
        name="fill",
    )(reg, *edges, tile, sky, grp, lan, obsm)


def by_lane_tile(x):
    return x.reshape(2, NPHI // 128, 128).transpose(1, 0, 2)


def shifted(x, d):
    return lax.ppermute(x, "reg", [(i, (i + d) % NREG) for i in range(NREG)])


def body(coefficients, legendre, harmonic_orders, observed, hole_rows, boundary, tile_owner, kriging):
    reg = lax.axis_index("reg").astype(I32).reshape(1)
    sums = legendre_sums(legendre, coefficients)
    spectra = lax.all_to_all(sums, "blk", split_axis=0, concat_axis=0, tiled=True).reshape(NK, 128)
    pb, ph, obsb, grp, lan, obsm = prepare(
        reg, by_lane_tile(hole_rows), by_lane_tile(observed), boundary.reshape(NREG, NB), harmonic_orders.reshape(1, -1)
    )
    tile = kriging.reshape(HMAX, NB)
    tiles = [tile] + [shifted(tile, d) for d in (1, 2, 3)]
    away = residuals(spectra, pb, obsb)
    edges = [shifted(x, d + 1) for d, x in enumerate(away)]
    sky, my_tile, own = hole_sky(reg, tile_owner, spectra, ph, pb, obsb, tiles, away[2])
    out = fill(reg, [own] + edges, my_tile, sky, grp, lan, obsm)
    return out.reshape(NS, NPHI // 128, 2, 128).transpose(0, 2, 1, 3).reshape(NS, 2, NPHI)


def solution(mesh):
    return jax.shard_map(
        body,
        mesh=mesh,
        in_specs=(
            P("blk", None, None),
            P("blk", None, "reg", None, None),
            P(),
            P(("blk", "reg"), None),
            P(("blk", "reg"), None),
            P("blk", None, None),
            P("blk", None),
            P("blk", "reg", None, None),
        ),
        out_specs=P(None, ("blk", "reg"), None),
        check_vma=False,
    )
```

```python
import functools

import jax
import jax.numpy as jnp
from jax import lax
from jax.experimental import pallas as pl
from jax.experimental.pallas import tpu as pltpu
from jax.sharding import PartitionSpec as P

BF = jnp.bfloat16
F32 = jnp.float32
I32 = jnp.int32
NBLK = 64
NREG = 4
NM = 4
L = 2048
KT = L // 128
NPHI = 4096
NT = NPHI // 128
NG = 2 * NT
NB = 256
SLOTS = NB // NREG
HMAX = 512
NS = 128
NK = NBLK * 16
MB = 1024 * 1024
ROUND = 12582912.0
COS = (
    0.9999999890590234,
    -19.739204499453898,
    64.93911745989367,
    -85.45013953084099,
    60.16763095056212,
    -25.967599246900118,
    6.528658158989,
)


def vmem():
    return pl.BlockSpec(memory_space=pltpu.VMEM)


def smem():
    return pl.BlockSpec(memory_space=pltpu.SMEM)


def anywhere():
    return pl.BlockSpec(memory_space=pl.ANY)


def params(mib):
    return pltpu.CompilerParams(vmem_limit_bytes=mib * MB)


def iota(shape, axis):
    return lax.broadcasted_iota(I32, shape, axis)


def dot(a, b):
    return jnp.dot(a, b, preferred_element_type=F32)


def dot_nt(a, b):
    return lax.dot_general(a, b, (((1,), (1,)), ((), ())), preferred_element_type=F32)


STEPS = 8
WIDE = KT // STEPS
DEEP = L // STEPS


def legendre_kernel(leg, coef, out, legv, coefv, lsem, csem):
    def coef_copy(k):
        at = pl.ds(k * DEEP, DEEP)
        return pltpu.make_async_copy(coef.at[:, at], coefv.at[:, at], csem.at[k])

    for k in range(STEPS):
        for t in range(k * WIDE, (k + 1) * WIDE):
            pltpu.make_async_copy(leg.at[:, :, t], legv.at[t], lsem.at[k]).start()
        coef_copy(k).start()
    totals = [jnp.zeros((2 * NBLK, 2 * NS), F32)] * NM
    for k in range(STEPS):
        part = legv.at[k * WIDE : (k + 1) * WIDE]
        pltpu.make_async_copy(part, part, lsem.at[k]).wait()
        coef_copy(k).wait()
        for m in range(NM):
            left = [legv.at[t, m].reshape(2 * NBLK, 128)[...] for t in range(k * WIDE, (k + 1) * WIDE)]
            totals[m] += dot(jnp.concatenate(left, axis=1), coefv[m, k * DEEP : (k + 1) * DEEP, :])
    for m in range(NM):
        rounded = totals[m].astype(BF)
        for c in range(2):
            out[:, c, m] = rounded[:, c * 128 : (c + 1) * 128].reshape(NBLK, 2, 128)


def legendre_sums(legendre, coefficients):
    view = legendre.reshape(NM, NBLK, 2, KT, 128).transpose(0, 1, 3, 2, 4)
    return pl.pallas_call(
        legendre_kernel,
        out_shape=jax.ShapeDtypeStruct((NBLK, 2, NM, 2, 128), BF),
        in_specs=[anywhere(), anywhere()],
        out_specs=vmem(),
        scratch_shapes=[
            pltpu.VMEM((KT, NM, NBLK, 2, 128), BF),
            pltpu.VMEM((NM, L, 2 * NS), BF),
            pltpu.SemaphoreType.DMA((STEPS,)),
            pltpu.SemaphoreType.DMA((STEPS,)),
        ],
        compiler_params=params(62),
        cost_estimate=pl.CostEstimate(flops=2 * NM * 128 * L * 256, bytes_accessed=6 * MB, transcendentals=0),
        name="legendre_sums",
    )(view, coefficients)


def prepare_kernel(reg, holes, observed, boundary, orders, pb, ph, obsb, grp, lan, obsm, amat, bmat, pcol, rcol, rows):
    me = reg[0]
    h = holes[...].reshape(NG, 128)
    obs = observed[...].reshape(NG, 128)
    obsm[...] = jnp.where(h >= 0, 0.0, obs).astype(BF)

    hi, lo = h >> 4, h & 15
    a_iota, b_iota, lane = iota((32, 128), 0), iota((16, 128), 0), iota((32, 128), 1).astype(F32)
    for g in range(NG):
        hit = a_iota == hi[g : g + 1, :]
        at = pl.ds(g * 128, 128)
        amat[0:32, at] = jnp.where(hit, float(g + 1), 0.0).astype(BF)
        amat[32:64, at] = jnp.where(hit, lane, 0.0).astype(BF)
        bmat[:, at] = jnp.where(b_iota == lo[g : g + 1, :], 1.0, 0.0).astype(BF)
    tall = dot_nt(amat[...], bmat[...]).astype(BF)
    wide = dot_nt(bmat[...], amat[...]).astype(BF)
    pick = (iota((HMAX, 32), 0) // 16 == iota((HMAX, 32), 1)).astype(F32).astype(BF)
    low = iota((HMAX, 16), 0) % 16 == iota((HMAX, 16), 1)
    g1 = jnp.sum(jnp.where(low, dot(pick, tall[0:32]), 0.0), axis=1, keepdims=True)
    lh = jnp.sum(jnp.where(low, dot(pick, tall[32:64]), 0.0), axis=1, keepdims=True)
    pick_t = (iota((32, HMAX), 1) // 16 == iota((32, HMAX), 0)).astype(F32).astype(BF)
    low_t = iota((16, HMAX), 1) % 16 == iota((16, HMAX), 0)
    g1_row = jnp.sum(jnp.where(low_t, dot(wide[:, 0:32], pick_t), 0.0), axis=0, keepdims=True)
    grp[...] = jnp.where(iota((NT, HMAX), 0).astype(F32) == jnp.floor((g1_row - 1.0) * 0.5), 1.0, 0.0).astype(BF)
    gh = g1 - 1.0
    tile_h = jnp.floor(gh * 0.5)
    place = (gh - 2.0 * tile_h) * 128.0 + lh
    lan[...] = jnp.where(iota((HMAX, 256), 1).astype(F32) == place, 1.0, 0.0).astype(BF)
    pcol[NB:, :] = jnp.broadcast_to(tile_h * 128.0 + lh, (HMAX, 128))
    rcol[NB:, :] = jnp.broadcast_to(gh - 2.0 * tile_h, (HMAX, 128))

    mine = iota((SLOTS, NB), 1) == iota((SLOTS, NB), 0) + me * SLOTS
    cols = []
    for d in range(NREG):
        line = boundary[pl.ds(lax.rem(me + d, NREG), 1), :].astype(F32)
        cols.append(jnp.sum(jnp.where(mine, line, 0.0), axis=1, keepdims=True))
    u = jnp.concatenate(cols, axis=0) - (me * (2 * NPHI)).astype(F32)
    rb = jnp.where(u >= float(NPHI), 1.0, 0.0)
    p = u - rb * float(NPHI)
    tile_b = jnp.floor(p * (1.0 / 128.0))
    lane_b = p - tile_b * 128.0
    pcol[0:NB, :] = jnp.broadcast_to(p, (NB, 128))
    rcol[0:NB, :] = jnp.broadcast_to(rb, (NB, 128))
    one = jnp.where(iota((NB, NG), 1).astype(F32) == 2.0 * tile_b + rb, 1.0, 0.0).astype(BF)
    first = obs.astype(BF)
    rest = obs - first.astype(F32)
    second = rest.astype(BF)
    third = (rest - second.astype(F32)).astype(BF)
    value = dot(one, first) + dot(one, second) + dot(one, third)
    value = jnp.where(iota((NB, 128), 1).astype(F32) == lane_b, value, 0.0)
    obsb[...] = jnp.broadcast_to(jnp.sum(value, axis=1, keepdims=True), (NB, 128))

    line = jnp.broadcast_to(orders[...], (8, 256))
    split = jnp.concatenate([(line >> 3).astype(F32), (line & 7).astype(F32)], axis=0).astype(BF)
    at = iota((256, NK), 1)
    spread = (iota((256, NK), 0) == (at >> 4) * 4 + ((at & 7) >> 1)).astype(F32).astype(BF)
    both = dot(split, spread)
    order = both[0:8] * 8.0 + both[8:16]
    at = iota((8, NK), 1)
    rows[0] = order * (1.0 / NPHI)
    rows[1] = ((at >> 3) & 1).astype(F32) * 0.25
    rows[2] = (at & 1).astype(F32)
    rows[3] = jnp.where(order == 0.0, 1.0, 2.0)

    def phases(out, base):
        def step(i, _):
            at = pl.multiple_of(i * 16, 16)
            pc = pcol[pl.ds(base + at, 16), :]
            rc = rcol[pl.ds(base + at, 16), :]
            for t in range(NK // 128):
                ls = slice(t * 128, (t + 1) * 128)
                turn = pc * rows[0, 0:1, ls] + rows[1, 0:1, ls]
                turn = turn - ((turn + ROUND) - ROUND)
                z = turn * turn
                value = jnp.full((16, 128), COS[-1], F32)
                for c in COS[-2::-1]:
                    value = value * z + c
                weight = jnp.where(rc == rows[2, 0:1, ls], rows[3, 0:1, ls], 0.0)
                out[pl.ds(at, 16), ls] = (value * weight).astype(BF)
            return 0

        lax.fori_loop(0, out.shape[0] // 16, step, 0)

    phases(pb, 0)
    phases(ph, NB)


def prepare(reg, holes, observed, boundary, orders):
    shapes = [
        ((NB, NK), BF),
        ((HMAX, NK), BF),
        ((NB, 128), F32),
        ((NT, HMAX), BF),
        ((HMAX, 256), BF),
        ((NG, 128), BF),
    ]
    return pl.pallas_call(
        prepare_kernel,
        out_shape=[jax.ShapeDtypeStruct(s, t) for s, t in shapes],
        in_specs=[smem()] + [vmem()] * 4,
        out_specs=[vmem()] * 6,
        scratch_shapes=[
            pltpu.VMEM((64, 2 * NPHI), BF),
            pltpu.VMEM((16, 2 * NPHI), BF),
            pltpu.VMEM((NB + HMAX, 128), F32),
            pltpu.VMEM((NB + HMAX, 128), F32),
            pltpu.VMEM((4, 8, NK), F32),
        ],
        compiler_params=params(30),
        cost_estimate=pl.CostEstimate(flops=20_000_000, bytes_accessed=8 * MB, transcendentals=0),
        name="prepare",
    )(reg, holes, observed, boundary, orders)


def residual_kernel(spectra, pb, obsb, own, to1, to2, to3):
    sky = dot(pb[...], spectra[...]).astype(BF).astype(F32)
    residual = (obsb[...] - sky).astype(BF)
    for d, ref in enumerate((own, to1, to2, to3)):
        ref[...] = residual[d * SLOTS : (d + 1) * SLOTS, :]


def residuals(spectra, pb, obsb):
    return pl.pallas_call(
        residual_kernel,
        out_shape=[jax.ShapeDtypeStruct((SLOTS, NS), BF)] * NREG,
        in_specs=[vmem()] * 3,
        out_specs=[vmem()] * NREG,
        compiler_params=params(30),
        cost_estimate=pl.CostEstimate(flops=2 * NB * NK * NS, bytes_accessed=MB, transcendentals=0),
        name="residuals",
    )(spectra, pb, obsb)


def hole_kernel(reg, owners, spectra, ph, tile0, tile1, tile2, tile3, after, sky, tile):
    del after
    sky[...] = dot(ph[...], spectra[...]).T.astype(BF)
    me = reg[0]
    away = lax.rem(me - owners[0, me] + NREG, NREG)
    for d, ref in enumerate((tile0, tile1, tile2, tile3)):

        @pl.when(away == d)
        def _(ref=ref):
            tile[...] = ref[...].T


def hole_sky(reg, owners, spectra, ph, tiles, after):
    return pl.pallas_call(
        hole_kernel,
        out_shape=[jax.ShapeDtypeStruct((NS, HMAX), BF), jax.ShapeDtypeStruct((NB, HMAX), BF)],
        in_specs=[smem(), smem()] + [vmem()] * 6 + [anywhere()],
        out_specs=[vmem()] * 2,
        compiler_params=params(30),
        cost_estimate=pl.CostEstimate(flops=2 * HMAX * NK * NS, bytes_accessed=2 * MB, transcendentals=0),
        name="hole_sky",
    )(reg, owners, spectra, ph, *tiles, after)


CHUNK = 8


def fill_kernel(reg, own, from1, from2, from3, tile, sky, grp, lan, obsm, out, edge, xt, outv, sem):
    me = reg[0]
    for d, ref in enumerate((own, from1, from2, from3)):
        source = lax.rem(me - d + NREG, NREG)
        edge[pl.ds(pl.multiple_of(source * SLOTS, SLOTS), SLOTS), :] = ref[...]
    correction = dot(edge[...].T, tile[...]).astype(BF)
    xt[...] = (sky[...].astype(F32) + correction.astype(F32)).astype(BF).astype(F32)
    groups = grp[...]
    lanes = lan[...]
    base = obsm[...].astype(F32)

    def copy(i):
        at = pl.ds(i * CHUNK * NG, CHUNK * NG)
        return pltpu.make_async_copy(outv.at[at], out.at[at], sem)

    for i in range(NS // CHUNK):
        lines = xt[i * CHUNK : (i + 1) * CHUNK, :].astype(BF)
        left = lines[:, None, :] * groups[None]
        got = dot(left.reshape(CHUNK * NT, HMAX), lanes)
        got = got.reshape(CHUNK * NG, 128)
        for j in range(CHUNK):
            at = i * CHUNK * NG + j * NG
            outv[at : at + NG, :] = (got[j * NG : (j + 1) * NG, :] + base).astype(BF)
        copy(i).start()
    pltpu.make_async_copy(outv, outv, sem).wait()


def fill(reg, edges, tile, sky, grp, lan, obsm):
    return pl.pallas_call(
        fill_kernel,
        out_shape=jax.ShapeDtypeStruct((NS * NG, 128), BF),
        in_specs=[smem()] + [vmem()] * 9,
        out_specs=anywhere(),
        scratch_shapes=[
            pltpu.VMEM((NB, NS), BF),
            pltpu.VMEM((NS, HMAX), F32),
            pltpu.VMEM((NS * NG, 128), BF),
            pltpu.SemaphoreType.DMA,
        ],
        compiler_params=params(16),
        cost_estimate=pl.CostEstimate(flops=2 * NS * NG * HMAX * 128, bytes_accessed=3 * MB, transcendentals=0),
        name="fill",
    )(reg, *edges, tile, sky, grp, lan, obsm)


def by_lane_tile(x):
    return x.reshape(2, NPHI // 128, 128).transpose(1, 0, 2)


def shifted(x, d):
    return lax.ppermute(x, "reg", [(i, (i + d) % NREG) for i in range(NREG)])


def body(coefficients, legendre, harmonic_orders, observed, hole_rows, boundary, tile_owner, kriging):
    reg = lax.axis_index("reg").astype(I32).reshape(1)
    sums = legendre_sums(legendre, coefficients)
    spectra = lax.all_to_all(sums, "blk", split_axis=0, concat_axis=0, tiled=True).reshape(NK, 128)
    pb, ph, obsb, grp, lan, obsm = prepare(
        reg, by_lane_tile(hole_rows), by_lane_tile(observed), boundary.reshape(NREG, NB), harmonic_orders.reshape(1, -1)
    )
    tile = kriging.reshape(HMAX, NB)
    tiles = [tile] + [shifted(tile, d) for d in (1, 2, 3)]
    own, *away = residuals(spectra, pb, obsb)
    edges = [own] + [shifted(x, d + 1) for d, x in enumerate(away)]
    sky, my_tile = hole_sky(reg, tile_owner, spectra, ph, tiles, own)
    out = fill(reg, edges, my_tile, sky, grp, lan, obsm)
    return out.reshape(NS, NPHI // 128, 2, 128).transpose(0, 2, 1, 3).reshape(NS, 2, NPHI)


def solution(mesh):
    return jax.shard_map(
        body,
        mesh=mesh,
        in_specs=(
            P("blk", None, None),
            P("blk", None, "reg", None, None),
            P(),
            P(("blk", "reg"), None),
            P(("blk", "reg"), None),
            P("blk", None, None),
            P("blk", None),
            P("blk", "reg", None, None),
        ),
        out_specs=P(None, ("blk", "reg"), None),
        check_vma=False,
    )
```
